512 devices in a mesh: orb: 128 (over z, y, core), grp: 4 (over x).
Axes of the slice: x: 4, y: 8, z: 8, core: 2. Of those that a mesh axis runs over, the one named last changes fastest.
Arguments:
- orbitals: float32 [768, 2, 32, 1024], P('orb', None, 'grp'), may hold values from -6 to 6
- box_offsets: int32 [3, 768], replicated, may hold values from 0 to 191, as said below
- pair_first: int32 [128, 4, 2], P('orb', 'grp'), may hold values from 0 to 767, as said below
- pair_second: int32 [128, 4, 2], P('orb', 'grp'), may hold values from 0 to 767, as said below
- pair_count: int32 [128, 4], P('orb', 'grp'), may hold values from 1 to 2, as said below
Outputs:
- exchange: float32 [768, 2, 32, 1024], P('orb', None, 'grp')
The draws below stay inside these ranges and needn't reach their ends.
Inputs may be any that keep to these rules, and one draw needn't show every extreme that they name: `box_offsets`: each component of the periodic difference of two orbitals' offsets, taken as in the first step, is under 32 // 2 in magnitude. pair_first[o, g, s] is an orbital of block o, that is of o * 6 to o * 6 + 5. pair_second[o, g, s] is an orbital of block o, not below pair_first, or of block (o + 1) mod 128. Over all live slots every unordered pair stands at most once. `pair_count`: in every block one device has all 2 slots live.
All inputs are finite; a program needn't handle non-finite values.
Results may differ from the reference program's by a relative error of at most 0.0003.
Values sent between devices are 32-bit elements; how exact they have to be, the bound alone decides.
No kernel may reach another device: no remote copies, remote signals or barrier semaphores. Data moves between devices by JAX's collectives and lax.ppermute only.
A program may use at most 64 MiB of HBM per device.

```python
import jax
import jax.numpy as jnp
import numpy as np
from jax import lax

BOX = 32
CELLS = 1024
GRID = 192
ORB_DEV = 6
PAIRS_DEV = 2
ORBITALS = 768
N_ORB = 128
N_GRP = 4


def pair_tables(key):
    near_first = []
    near_second = []
    for first in range(ORB_DEV):
        for second in range(first, ORB_DEV):
            near_first.append(first)
            near_second.append(second)
    for first in range(ORB_DEV):
        for second in range(ORB_DEV):
            near_first.append(first)
            near_second.append(ORB_DEV + second)
    first_table = jnp.array(np.array(near_first, dtype=np.int32))
    second_table = jnp.array(np.array(near_second, dtype=np.int32))
    per_block = len(near_first)
    keys = jax.random.split(key, N_ORB)
    order = jax.vmap(lambda block_key: jax.random.permutation(block_key, per_block))(keys)
    order = order[:, :N_GRP * PAIRS_DEV]
    pick_first = first_table[order]
    pick_second = second_table[order]
    block = jnp.arange(N_ORB, dtype=jnp.int32)[:, None]
    first = block * ORB_DEV + pick_first
    second = (block + pick_second // ORB_DEV) % N_ORB * ORB_DEV + pick_second % ORB_DEV
    return (first.reshape(N_ORB, N_GRP, PAIRS_DEV), second.reshape(N_ORB, N_GRP, PAIRS_DEV))


def draw_pair_first(key, part):
    return pair_tables(key)[0].astype(jnp.int32)


def draw_pair_second(key, part):
    return pair_tables(key)[1].astype(jnp.int32)


def draw_pair_count(key, part):
    key = jax.random.fold_in(key, 5)
    key_full, key_rest = jax.random.split(key)
    full = jax.random.randint(key_full, (N_ORB,), 0, N_GRP)
    rest = jax.random.randint(key_rest, (N_ORB, N_GRP), 1, PAIRS_DEV + 1)
    members = jnp.arange(N_GRP, dtype=jnp.int32)[None, :]
    return jnp.where(members == full[:, None], PAIRS_DEV, rest).astype(jnp.int32)


def draw_box_offsets(key, part):
    key = jax.random.fold_in(key, 3)
    rel = jax.random.randint(key, (3, ORBITALS), 0, BOX // 2)
    rel = rel.at[:, 0].set(0)
    rel = rel.at[:, 1].set(1)
    return ((GRID - 1 + rel) % GRID).astype(jnp.int32)


def steps_of(stream_key, shape, shards, smallest, largest):
    def one(axis_at, shards_of):
        heights = jax.random.uniform(jax.random.fold_in(jax.random.fold_in(stream_key, 6), axis_at), (shards_of,), jnp.float32, smallest / len(shards), largest / len(shards))
        return jnp.repeat(jnp.exp(heights), shape[axis_at] // shards_of).reshape((-1,) + (1,) * (len(shape) - axis_at - 1))

    level = one(*shards[0])
    for cut in shards[1:]:
        level = level * one(*cut)
    return level


def gaussian(own_key, dims, scale, reach, cuts=(), kind=jnp.bfloat16):
    loudness = steps_of(own_key, dims, cuts, -0.22, 0.18) if cuts else 1.0
    values = jax.random.normal(own_key, dims, jnp.float32) * scale * loudness
    return jnp.minimum(jnp.maximum(values, -reach), reach).astype(kind)


def setup_inputs(seed: int = 0) -> dict:
    splits = jax.random.split(jax.random.key(seed), 6)
    return {
        "orbitals": gaussian(splits[0], (ORBITALS, 2, BOX, CELLS), 1.0, 6.0, ((0, 128), (2, 4)), jnp.float32),
        "box_offsets": draw_box_offsets(jax.random.fold_in(splits[5], 71), 0),
        "pair_first": draw_pair_first(jax.random.fold_in(splits[5], 71), 0),
        "pair_second": draw_pair_second(jax.random.fold_in(splits[5], 71), 0),
        "pair_count": draw_pair_count(jax.random.fold_in(splits[5], 71), 0),
    }


SCREEN = 0.5


def green_cube():
    modes = jnp.arange(BOX, dtype=jnp.float32)
    lam = (2.0 * jnp.sin(jnp.pi * modes / BOX)) ** 2
    return 1.0 / (SCREEN + lam[:, None, None] + lam[None, :, None] + lam[None, None, :])


def carry_box(field, move):
    padded = jnp.pad(field, ((0, 0), (BOX, BOX), (BOX, BOX), (BOX, BOX)))
    zero = jnp.zeros((), jnp.int32)
    starts = (zero, (BOX - move[0]).astype(jnp.int32), (BOX - move[1]).astype(jnp.int32), (BOX - move[2]).astype(jnp.int32))
    return lax.dynamic_slice(padded, starts, (2, BOX, BOX, BOX))


def reference(orbitals, box_offsets, pair_first, pair_second, pair_count):
    boxes = orbitals.reshape(ORBITALS, 2, BOX, BOX, BOX)
    firsts = pair_first.reshape(-1)
    seconds = pair_second.reshape(-1)
    slots = jnp.arange(PAIRS_DEV, dtype=jnp.int32)
    live = (slots[None, None, :] < pair_count[:, :, None]).reshape(-1)
    green = green_cube()

    def step(total, item):
        first, second, alive = item
        move = (box_offsets[:, second] - box_offsets[:, first] + GRID // 2) % GRID - GRID // 2
        phi_first = boxes[first]
        moved = carry_box(boxes[second], move)
        rho_re = moved[0] * phi_first[0] + moved[1] * phi_first[1]
        rho_im = moved[0] * phi_first[1] - moved[1] * phi_first[0]
        freq = jnp.fft.fftn(lax.complex(rho_re, rho_im))
        pot = jnp.fft.ifftn(green * freq)
        pot_re = jnp.real(pot)
        pot_im = jnp.imag(pot)
        to_first = jnp.stack([moved[0] * pot_re - moved[1] * pot_im, moved[0] * pot_im + moved[1] * pot_re])
        on_first = jnp.stack([phi_first[0] * pot_re + phi_first[1] * pot_im, phi_first[1] * pot_re - phi_first[0] * pot_im])
        to_second = carry_box(on_first, -move)
        weight_first = alive.astype(total.dtype)
        weight_second = (alive & (first != second)).astype(total.dtype)
        total = total.at[first].add(weight_first * to_first)
        total = total.at[second].add(weight_second * to_second)
        return total, None

    total, _ = lax.scan(step, jnp.zeros(boxes.shape, jnp.float32), (firsts, seconds, live))
    return (-total).reshape(ORBITALS, 2, BOX, CELLS)
```

```python
import jax
import jax.numpy as jnp
import ml_dtypes
import numpy as np
from jax import lax
from jax.experimental import pallas as pl
from jax.experimental.pallas import tpu as pltpu
from jax.sharding import PartitionSpec as P

BOX = 32
CELLS = 1024
GRID = 192
ORB_DEV = 6
PAIRS = 2
SCREEN = 0.5
LANES = 128
SLABS = CELLS // LANES
PARTS = LANES // BOX
ROWS = SLABS * BOX
PAD_SLABS = 4
PAD_ROWS = 16
F32 = jnp.float32
BF16 = jnp.bfloat16


def split_bf16(table):
    high = table.astype(ml_dtypes.bfloat16)
    low = (table - high.astype(np.float64)).astype(ml_dtypes.bfloat16)
    return high, low


def make_tables():
    slab, x = np.divmod(np.arange(ROWS), BOX)
    part, z = np.divmod(np.arange(LANES), BOX)
    left = np.exp(-2j * np.pi * (np.outer(slab, slab) / SLABS + np.outer(x, x) / BOX))
    right = np.exp(-2j * np.pi * (np.outer(part, part) / PARTS + np.outer(z, z) / BOX))
    twiddle = np.exp(-2j * np.pi * np.outer(np.arange(SLABS), part) / BOX)
    left_high, left_low = split_bf16(np.concatenate([left.real, left.imag], 0))
    left3 = np.concatenate([left_high, left_high, left_low], 1)
    forward = np.block([[right.real, right.imag], [-right.imag, right.real]])
    for_high, for_low = split_bf16(forward)
    for3 = np.concatenate([for_high, for_high, for_low], 0)
    back_high, back_low = split_bf16(forward.T)
    back3 = np.concatenate([back_high, back_high, back_low], 0)
    lam = (2.0 * np.sin(np.pi * np.arange(BOX) / BOX)) ** 2
    lam_row = lam[x][:, None]
    lam_y = lam[slab[:, None] + SLABS * part[None, :]]
    green = 1.0 / (SCREEN + lam_row + lam_y + lam[z][None, :]) / float(BOX**3)
    return (
        left3,
        for3,
        back3,
        twiddle.real.astype(np.float32),
        twiddle.imag.astype(np.float32),
        green.astype(np.float32),
    )


TABLES = make_tables()


def from_behind(value, axis, steps):
    count = lax.axis_size(axis)
    pairs = [(source, (source + steps) % count) for source in range(count)]
    return lax.ppermute(value, axis, pairs)


def places(lists, who, turn):
    first = lists[who, turn]
    second = lists[who, PAIRS + turn]
    ahead = (first // ORB_DEV) != (second // ORB_DEV)
    return first % ORB_DEV, second % ORB_DEV, ahead, first != second


def pack_kernel(lists, own, ahead, send, sem):
    members = send.shape[0]
    for who in range(members):
        for turn in range(PAIRS):
            at_first, at_second, is_ahead, _ = places(lists, who, turn)
            pltpu.make_async_copy(own.at[at_first], send.at[who, 2 * turn], sem).start()

            @pl.when(is_ahead)
            def _():
                pltpu.make_async_copy(ahead.at[at_second], send.at[who, 2 * turn + 1], sem).start()

            @pl.when(jnp.logical_not(is_ahead))
            def _():
                pltpu.make_async_copy(own.at[at_second], send.at[who, 2 * turn + 1], sem).start()

    pltpu.make_async_copy(send, send, sem).wait()


def split3(value):
    high = value.astype(BF16)
    low = (value - high.astype(F32)).astype(BF16)
    return high, low


def dot(a, b):
    return jnp.dot(a, b, preferred_element_type=F32)


def left_product(left3, re, im):
    high, low = split3(jnp.concatenate([re, im], 1))
    both = dot(left3[...], jnp.concatenate([high, low, high], 0))
    return both[:ROWS, :LANES], both[:ROWS, LANES:], both[ROWS:, :LANES], both[ROWS:, LANES:]


def right_product(re, im, table):
    high, low = split3(jnp.concatenate([re, im], 1))
    both = dot(jnp.concatenate([high, low, high], 1), table[...])
    return both[:, :LANES], both[:, LANES:]


def by_rows(table):
    return jnp.concatenate(
        [jnp.broadcast_to(table[slab : slab + 1, :], (BOX, LANES)) for slab in range(SLABS)], 0
    )


def poisson(re, im, left3, for3, back3, twid_re, twid_im, green):
    rr, ri, ir, ii = left_product(left3, re, im)
    a_re, a_im = rr - ii, ri + ir
    w_re, w_im = by_rows(twid_re), by_rows(twid_im)
    b_re, b_im = a_re * w_re - a_im * w_im, a_re * w_im + a_im * w_re
    f_re, f_im = right_product(b_re, b_im, for3)
    weight = green[...]
    c_re, c_im = right_product(f_re * weight, f_im * weight, back3)
    d_re, d_im = c_re * w_re + c_im * w_im, c_im * w_re - c_re * w_im
    rr, ri, ir, ii = left_product(left3, d_re, d_im)
    return rr + ii, ri - ir


def shifted(tile_of, buf, move):
    flat = move[1] * BOX + move[2]
    slabs = flat >> 7
    turn = flat & (LANES - 1)
    for comp in range(2):
        for slab in range(SLABS):
            rolled = pltpu.roll(tile_of(comp, slab), turn, 1)
            buf[comp, PAD_SLABS + slab, PAD_ROWS : PAD_ROWS + BOX, :] = rolled
    lane = lax.broadcasted_iota(jnp.int32, (BOX, LANES), 1)
    row = lax.broadcasted_iota(jnp.int32, (BOX, LANES), 0) - move[0]
    zcell = (lane & (BOX - 1)) - move[2]
    part = (lane >> 5) - move[1]
    base = (row >= 0) & (row < BOX) & (zcell >= 0) & (zcell < BOX)
    straight = lane >= turn
    out = []
    for comp in range(2):
        tiles = []
        for slab in range(SLABS + 1):
            tiles.append(buf[comp, PAD_SLABS - 1 + slab - slabs, pl.ds(PAD_ROWS - move[0], BOX), :])
        parts = []
        for slab in range(SLABS):
            ycell = part + slab * PARTS
            keep = base & (ycell >= 0) & (ycell < BOX)
            picked = jnp.where(straight, tiles[slab + 1], tiles[slab])
            parts.append(jnp.where(keep, picked, 0.0))
        out.append(jnp.concatenate(parts, 0))
    return out


def pair_kernel(
    offsets, firsts, seconds, got, left3, for3, back3, twid_re, twid_im, green, send, *bufs
):
    members = got.shape[0]
    height = BOX // members

    def field_tile(slot, comp, slab):
        lanes = slice(slab * LANES, (slab + 1) * LANES)
        return jnp.concatenate([got[who, slot, comp, :, lanes] for who in range(members)], 0)

    def field(slot, comp):
        return jnp.concatenate([field_tile(slot, comp, slab) for slab in range(SLABS)], 0)

    def put(slot, comp, value):
        for slab in range(SLABS):
            for who in range(members):
                at = slab * BOX + who * height
                send[who, slot, comp, :, slab * LANES : (slab + 1) * LANES] = value[at : at + height]

    for turn in range(PAIRS):
        buf = bufs[turn]
        first = firsts[0, 0, turn]
        second = seconds[0, 0, turn]
        move = []
        for axis in range(3):
            gap = offsets[axis, second] - offsets[axis, first] + GRID // 2
            gap = jnp.where(gap < 0, gap + GRID, gap)
            gap = jnp.where(gap >= GRID, gap - GRID, gap)
            move.append(gap - GRID // 2)
        m_re, m_im = shifted(lambda comp, slab: field_tile(2 * turn + 1, comp, slab), buf, move)
        f_re, f_im = field(2 * turn, 0), field(2 * turn, 1)
        rho_re = m_re * f_re + m_im * f_im
        rho_im = m_re * f_im - m_im * f_re
        p_re, p_im = poisson(rho_re, rho_im, left3, for3, back3, twid_re, twid_im, green)
        put(2 * turn, 0, m_re * p_re - m_im * p_im)
        put(2 * turn, 1, m_re * p_im + m_im * p_re)
        back = (f_re * p_re + f_im * p_im, f_im * p_re - f_re * p_im)
        s_re, s_im = shifted(
            lambda comp, slab: back[comp][slab * BOX : (slab + 1) * BOX], buf, [-step for step in move]
        )
        put(2 * turn + 1, 0, s_re)
        put(2 * turn + 1, 1, s_im)


def ahead_kernel(lists, got, out):
    out[...] = jnp.zeros(out.shape, F32)
    for who in range(got.shape[0]):
        for turn in range(PAIRS):
            _, at_second, is_ahead, _ = places(lists, who, turn)

            @pl.when(is_ahead & (turn < lists[who, 2 * PAIRS]))
            def _():
                out[at_second] -= got[who, 2 * turn + 1]


def own_kernel(lists, got, out):
    out[...] = jnp.zeros(out.shape, F32)
    for who in range(got.shape[0]):
        for turn in range(PAIRS):
            at_first, at_second, is_ahead, differs = places(lists, who, turn)
            live = turn < lists[who, 2 * PAIRS]

            @pl.when(live)
            def _():
                out[at_first] -= got[who, 2 * turn]

            @pl.when(live & differs & jnp.logical_not(is_ahead))
            def _():
                out[at_second] -= got[who, 2 * turn + 1]


def local(orbitals, box_offsets, pair_first, pair_second, pair_count):
    members = lax.axis_size("grp")
    rows = orbitals.shape[2]
    smem = pl.BlockSpec(memory_space=pltpu.SMEM)
    vmem = pl.BlockSpec(memory_space=pltpu.VMEM)
    anywhere = pl.BlockSpec(memory_space=pl.ANY)
    limit = pltpu.CompilerParams(vmem_limit_bytes=40 * 1024 * 1024)
    ahead = from_behind(orbitals, "orb", -1)
    mine = jnp.concatenate([pair_first[0, 0], pair_second[0, 0], pair_count[0]])
    lists = lax.all_gather(mine, "grp", axis=0)
    slots = 2 * PAIRS
    fields = jax.ShapeDtypeStruct((members, slots, 2, rows, CELLS), F32)
    packed = pl.pallas_call(
        pack_kernel,
        out_shape=fields,
        in_specs=[smem, anywhere, anywhere],
        out_specs=anywhere,
        scratch_shapes=[pltpu.SemaphoreType.DMA],
        compiler_params=limit,
        name="pack",
    )(lists, orbitals, ahead)
    got = lax.all_to_all(packed, "grp", 0, 0)
    tables = [jnp.asarray(table) for table in TABLES]
    buf = pltpu.VMEM((2, SLABS + 2 * PAD_SLABS, BOX + 2 * PAD_ROWS, LANES), F32)
    terms = pl.pallas_call(
        pair_kernel,
        out_shape=fields,
        in_specs=[smem] * 3 + [vmem] * 7,
        out_specs=vmem,
        scratch_shapes=[buf] * PAIRS,
        compiler_params=limit,
        name="pairs",
    )(box_offsets, pair_first, pair_second, got, *tables)
    returned = lax.all_to_all(terms, "grp", 0, 0)
    shape = jax.ShapeDtypeStruct(orbitals.shape, F32)
    ahead_terms = pl.pallas_call(
        ahead_kernel,
        out_shape=shape,
        in_specs=[smem, vmem],
        out_specs=vmem,
        compiler_params=limit,
        name="ahead_terms",
    )(lists, returned)
    back = from_behind(ahead_terms, "orb", 1)
    own_terms = pl.pallas_call(
        own_kernel,
        out_shape=shape,
        in_specs=[smem, vmem],
        out_specs=vmem,
        compiler_params=limit,
        name="own_terms",
    )(lists, returned)
    return own_terms + back


def solution(mesh):
    placed = (
        P("orb", None, "grp", None),
        P(),
        P("orb", "grp", None),
        P("orb", "grp", None),
        P("orb", "grp"),
    )
    return jax.shard_map(
        local, mesh=mesh, in_specs=placed, out_specs=P("orb", None, "grp", None), check_vma=False
    )
```

```python
import jax
import jax.numpy as jnp
import ml_dtypes
import numpy as np
from jax import lax
from jax.experimental import pallas as pl
from jax.experimental.pallas import tpu as pltpu
from jax.sharding import PartitionSpec as P

BOX = 32
CELLS = 1024
GRID = 192
ORB_DEV = 6
PAIRS = 2
SCREEN = 0.5
LANES = 128
SLABS = CELLS // LANES
PARTS = LANES // BOX
ROWS = SLABS * BOX
PAD_SLABS = 4
PAD_ROWS = 16
F32 = jnp.float32
BF16 = jnp.bfloat16


def split_bf16(table):
    high = table.astype(ml_dtypes.bfloat16)
    low = (table - high.astype(np.float64)).astype(ml_dtypes.bfloat16)
    return high, low


def make_tables():
    slab, x = np.divmod(np.arange(ROWS), BOX)
    part, z = np.divmod(np.arange(LANES), BOX)
    left = np.exp(-2j * np.pi * (np.outer(slab, slab) / SLABS + np.outer(x, x) / BOX))
    right = np.exp(-2j * np.pi * (np.outer(part, part) / PARTS + np.outer(z, z) / BOX))
    twiddle = np.exp(-2j * np.pi * np.outer(np.arange(SLABS), part) / BOX)
    left_high, left_low = split_bf16(np.concatenate([left.real, left.imag], 0))
    left3 = np.concatenate([left_high, left_high, left_low], 1)
    forward = np.block([[right.real, right.imag], [-right.imag, right.real]])
    for_high, for_low = split_bf16(forward)
    for3 = np.concatenate([for_high, for_high, for_low], 0)
    back_high, back_low = split_bf16(forward.T)
    back3 = np.concatenate([back_high, back_high, back_low], 0)
    lam = (2.0 * np.sin(np.pi * np.arange(BOX) / BOX)) ** 2
    lam_row = lam[x][:, None]
    lam_y = lam[slab[:, None] + SLABS * part[None, :]]
    green = 1.0 / (SCREEN + lam_row + lam_y + lam[z][None, :]) / float(BOX**3)
    return (
        left3,
        for3,
        back3,
        twiddle.real.astype(np.float32),
        twiddle.imag.astype(np.float32),
        green.astype(np.float32),
    )


TABLES = make_tables()


def from_behind(value, axis, steps):
    count = lax.axis_size(axis)
    pairs = [(source, (source + steps) % count) for source in range(count)]
    return lax.ppermute(value, axis, pairs)


def own_list(pair_first, pair_second, pair_count):
    spare = LANES - 2 * PAIRS - 1
    mine = jnp.pad(pair_first, ((0, 0), (0, 0), (0, LANES - PAIRS)))
    mine += jnp.pad(pair_second, ((0, 0), (0, 0), (PAIRS, LANES - 2 * PAIRS)))
    mine += jnp.pad(pair_count, ((0, 0), (2 * PAIRS, spare)))[None]
    return mine


def block_lists(mine, members):
    row = lax.broadcasted_iota(jnp.int32, (members, 1, LANES), 0)
    return lax.psum(jnp.where(row == lax.axis_index("grp"), mine, 0), "grp")


def places(lists, who, turn):
    first = lists[who, 0, turn]
    second = lists[who, 0, PAIRS + turn]
    ahead = (first // ORB_DEV) != (second // ORB_DEV)
    return first % ORB_DEV, second % ORB_DEV, ahead, first != second


def stage_kernel(source, out):
    pltpu.sync_copy(source, out)


def pack_kernel(lists, behind, here, send):
    for who in range(send.shape[0]):
        for turn in range(PAIRS):
            at_first, at_second, is_ahead, _ = places(lists, who, turn)
            send[who, 2 * turn] = behind[at_first]

            @pl.when(is_ahead)
            def _():
                send[who, 2 * turn + 1] = here[at_second]

            @pl.when(jnp.logical_not(is_ahead))
            def _():
                send[who, 2 * turn + 1] = behind[at_second]


def split3(value):
    high = value.astype(BF16)
    low = (value - high.astype(F32)).astype(BF16)
    return high, low


def dot(a, b):
    return jnp.dot(a, b, preferred_element_type=F32)


def left_product(left3, re, im):
    high, low = split3(jnp.concatenate([re, im], 1))
    both = dot(left3[...], jnp.concatenate([high, low, high], 0))
    return both[:ROWS, :LANES], both[:ROWS, LANES:], both[ROWS:, :LANES], both[ROWS:, LANES:]


def right_product(re, im, table):
    high, low = split3(jnp.concatenate([re, im], 1))
    both = dot(jnp.concatenate([high, low, high], 1), table[...])
    return both[:, :LANES], both[:, LANES:]


def by_rows(table):
    return jnp.concatenate(
        [jnp.broadcast_to(table[slab : slab + 1, :], (BOX, LANES)) for slab in range(SLABS)], 0
    )


def poisson(re, im, left3, for3, back3, twid_re, twid_im, green):
    rr, ri, ir, ii = left_product(left3, re, im)
    a_re, a_im = rr - ii, ri + ir
    w_re, w_im = by_rows(twid_re), by_rows(twid_im)
    b_re, b_im = a_re * w_re - a_im * w_im, a_re * w_im + a_im * w_re
    f_re, f_im = right_product(b_re, b_im, for3)
    weight = green[...]
    c_re, c_im = right_product(f_re * weight, f_im * weight, back3)
    d_re, d_im = c_re * w_re + c_im * w_im, c_im * w_re - c_re * w_im
    rr, ri, ir, ii = left_product(left3, d_re, d_im)
    return rr + ii, ri - ir


def shifted(tile_of, buf, move):
    flat = move[1] * BOX + move[2]
    slabs = flat >> 7
    turn = flat & (LANES - 1)
    for comp in range(2):
        for slab in range(SLABS):
            rolled = pltpu.roll(tile_of(comp, slab), turn, 1)
            buf[comp, PAD_SLABS + slab, PAD_ROWS : PAD_ROWS + BOX, :] = rolled
    lane = lax.broadcasted_iota(jnp.int32, (BOX, LANES), 1)
    row = lax.broadcasted_iota(jnp.int32, (BOX, LANES), 0) - move[0]
    zcell = (lane & (BOX - 1)) - move[2]
    part = (lane >> 5) - move[1]
    base = (row >= 0) & (row < BOX) & (zcell >= 0) & (zcell < BOX)
    straight = lane >= turn
    out = []
    for comp in range(2):
        tiles = []
        for slab in range(SLABS + 1):
            tiles.append(buf[comp, PAD_SLABS - 1 + slab - slabs, pl.ds(PAD_ROWS - move[0], BOX), :])
        parts = []
        for slab in range(SLABS):
            ycell = part + slab * PARTS
            keep = base & (ycell >= 0) & (ycell < BOX)
            picked = jnp.where(straight, tiles[slab + 1], tiles[slab])
            parts.append(jnp.where(keep, picked, 0.0))
        out.append(jnp.concatenate(parts, 0))
    return out


def pair_kernel(
    offsets, mine, got, left3, for3, back3, twid_re, twid_im, green, send, *bufs
):
    members = got.shape[0]
    height = BOX // members

    def field_tile(slot, comp, slab):
        lanes = slice(slab * LANES, (slab + 1) * LANES)
        return jnp.concatenate([got[who, slot, comp, :, lanes] for who in range(members)], 0)

    def field(slot, comp):
        return jnp.concatenate([field_tile(slot, comp, slab) for slab in range(SLABS)], 0)

    def put(slot, comp, value):
        for slab in range(SLABS):
            for who in range(members):
                at = slab * BOX + who * height
                send[who, slot, comp, :, slab * LANES : (slab + 1) * LANES] = value[at : at + height]

    for turn in range(PAIRS):
        buf = bufs[turn]
        first = mine[0, 0, turn]
        second = mine[0, 0, PAIRS + turn]
        move = []
        for axis in range(3):
            gap = offsets[axis, second] - offsets[axis, first] + GRID // 2
            gap = jnp.where(gap < 0, gap + GRID, gap)
            gap = jnp.where(gap >= GRID, gap - GRID, gap)
            move.append(gap - GRID // 2)
        m_re, m_im = shifted(lambda comp, slab: field_tile(2 * turn + 1, comp, slab), buf, move)
        f_re, f_im = field(2 * turn, 0), field(2 * turn, 1)
        rho_re = m_re * f_re + m_im * f_im
        rho_im = m_re * f_im - m_im * f_re
        p_re, p_im = poisson(rho_re, rho_im, left3, for3, back3, twid_re, twid_im, green)
        put(2 * turn, 0, m_re * p_re - m_im * p_im)
        put(2 * turn, 1, m_re * p_im + m_im * p_re)
        back = (f_re * p_re + f_im * p_im, f_im * p_re - f_re * p_im)
        s_re, s_im = shifted(
            lambda comp, slab: back[comp][slab * BOX : (slab + 1) * BOX], buf, [-step for step in move]
        )
        put(2 * turn + 1, 0, s_re)
        put(2 * turn + 1, 1, s_im)


def here_kernel(lists, got, out):
    out[...] = jnp.zeros(out.shape, F32)
    for who in range(got.shape[0]):
        for turn in range(PAIRS):
            _, at_second, is_ahead, _ = places(lists, who, turn)

            @pl.when(is_ahead & (turn < lists[who, 0, 2 * PAIRS]))
            def _():
                out[at_second] -= got[who, 2 * turn + 1]


def back_kernel(lists, got, out):
    out[...] = jnp.zeros(out.shape, F32)
    for who in range(got.shape[0]):
        for turn in range(PAIRS):
            at_first, at_second, is_ahead, differs = places(lists, who, turn)
            live = turn < lists[who, 0, 2 * PAIRS]

            @pl.when(live)
            def _():
                out[at_first] -= got[who, 2 * turn]

            @pl.when(live & differs & jnp.logical_not(is_ahead))
            def _():
                out[at_second] -= got[who, 2 * turn + 1]


def local(orbitals, box_offsets, pair_first, pair_second, pair_count):
    members = lax.axis_size("grp")
    rows = orbitals.shape[2]
    smem = pl.BlockSpec(memory_space=pltpu.SMEM)
    vmem = pl.BlockSpec(memory_space=pltpu.VMEM)
    anywhere = pl.BlockSpec(memory_space=pl.ANY)
    limit = pltpu.CompilerParams(vmem_limit_bytes=40 * 1024 * 1024)
    mine = from_behind(own_list(pair_first, pair_second, pair_count), "orb", 1)
    here = pl.pallas_call(
        stage_kernel,
        out_shape=jax.ShapeDtypeStruct(orbitals.shape, F32),
        in_specs=[pl.BlockSpec(memory_space=pltpu.HBM)],
        out_specs=vmem,
        compiler_params=limit,
        name="stage",
    )(pltpu.with_memory_space_constraint(orbitals, pltpu.HBM))
    behind = from_behind(here, "orb", 1)
    lists = block_lists(mine, members)
    slots = 2 * PAIRS
    fields = jax.ShapeDtypeStruct((members, slots, 2, rows, CELLS), F32)
    packed = pl.pallas_call(
        pack_kernel,
        out_shape=fields,
        in_specs=[smem, vmem, vmem],
        out_specs=vmem,
        compiler_params=limit,
        name="pack",
    )(lists, behind, here)
    got = lax.all_to_all(packed, "grp", 0, 0)
    tables = [jnp.asarray(table) for table in TABLES]
    buf = pltpu.VMEM((2, SLABS + 2 * PAD_SLABS, BOX + 2 * PAD_ROWS, LANES), F32)
    terms = pl.pallas_call(
        pair_kernel,
        out_shape=fields,
        in_specs=[smem] * 2 + [vmem] * 7,
        out_specs=vmem,
        scratch_shapes=[buf] * PAIRS,
        compiler_params=limit,
        name="pairs",
    )(box_offsets, mine, got, *tables)
    returned = lax.all_to_all(terms, "grp", 0, 0)
    shape = jax.ShapeDtypeStruct(orbitals.shape, F32)
    back_terms = pl.pallas_call(
        back_kernel,
        out_shape=shape,
        in_specs=[smem, vmem],
        out_specs=vmem,
        compiler_params=limit,
        name="back_terms",
    )(lists, returned)
    back = from_behind(back_terms, "orb", -1)
    here_terms = pl.pallas_call(
        here_kernel,
        out_shape=shape,
        in_specs=[smem, vmem],
        out_specs=vmem,
        compiler_params=limit,
        name="here_terms",
    )(lists, returned)
    return here_terms + back


def solution(mesh):
    placed = (
        P("orb", None, "grp", None),
        P(),
        P("orb", "grp", None),
        P("orb", "grp", None),
        P("orb", "grp"),
    )
    return jax.shard_map(
        local, mesh=mesh, in_specs=placed, out_specs=P("orb", None, "grp", None), check_vma=False
    )
```

```python
import jax
import jax.numpy as jnp
import ml_dtypes
import numpy as np
from jax import lax
from jax.experimental import pallas as pl
from jax.experimental.pallas import tpu as pltpu
from jax.sharding import PartitionSpec as P

BOX = 32
CELLS = 1024
GRID = 192
ORB_DEV = 6
PAIRS = 2
SCREEN = 0.5
LANES = 128
SLABS = CELLS // LANES
PARTS = LANES // BOX
ROWS = SLABS * BOX
PAD_SLABS = 4
PAD_ROWS = 16
F32 = jnp.float32
BF16 = jnp.bfloat16


def split_bf16(table):
    high = table.astype(ml_dtypes.bfloat16)
    low = (table - high.astype(np.float64)).astype(ml_dtypes.bfloat16)
    return high, low


def make_tables():
    slab, x = np.divmod(np.arange(ROWS), BOX)
    part, z = np.divmod(np.arange(LANES), BOX)
    left = np.exp(-2j * np.pi * np.outer(np.arange(BOX), np.arange(BOX)) / BOX)
    right = np.exp(-2j * np.pi * (np.outer(part, part) / PARTS + np.outer(z, z) / BOX))
    twiddle = np.exp(-2j * np.pi * np.outer(np.arange(SLABS), part) / BOX)
    left_high, left_low = split_bf16(np.concatenate([left.real, left.imag], 0))
    left3 = np.concatenate([left_high, left_high, left_low], 1)
    forward = np.block([[right.real, right.imag], [-right.imag, right.real]])
    for_high, for_low = split_bf16(forward)
    for3 = np.concatenate([for_high, for_high, for_low], 0)
    back_high, back_low = split_bf16(forward.T)
    back3 = np.concatenate([back_high, back_high, back_low], 0)
    lam = (2.0 * np.sin(np.pi * np.arange(BOX) / BOX)) ** 2
    lam_row = lam[x][:, None]
    lam_y = lam[slab[:, None] + SLABS * part[None, :]]
    green = 1.0 / (SCREEN + lam_row + lam_y + lam[z][None, :]) / float(BOX**3)
    return (
        left3,
        for3,
        back3,
        twiddle.real.astype(np.float32),
        twiddle.imag.astype(np.float32),
        green.astype(np.float32),
    )


TABLES = make_tables()


def from_behind(value, axis, steps):
    count = lax.axis_size(axis)
    pairs = [(source, (source + steps) % count) for source in range(count)]
    return lax.ppermute(value, axis, pairs)


def places(lists, who, turn):
    first = lists[who, 0, turn]
    second = lists[who, 0, PAIRS + turn]
    ahead = (first // ORB_DEV) != (second // ORB_DEV)
    return first % ORB_DEV, second % ORB_DEV, ahead, first != second


def entry_kernel(firsts, seconds, count, rows, table, here, sem):
    copy = pltpu.make_async_copy(rows, here, sem)
    copy.start()
    who = lax.broadcasted_iota(jnp.int32, table.shape, 0)
    lane = lax.broadcasted_iota(jnp.int32, table.shape, 2)
    value = jnp.where(lane == 2 * PAIRS, count[0, 0], 0)
    for turn in range(PAIRS):
        value = jnp.where(lane == turn, firsts[0, 0, turn], value)
        value = jnp.where(lane == PAIRS + turn, seconds[0, 0, turn], value)
    table[...] = jnp.where(who == lax.axis_index("grp"), value, 0)
    copy.wait()


def pack_here_kernel(lists, here, send):
    for who in range(send.shape[0]):
        for turn in range(PAIRS):
            _, at_second, is_ahead, _ = places(lists, who, turn)

            @pl.when(is_ahead)
            def _():
                send[who, 2 * turn + 1] = here[at_second]


def pack_behind_kernel(lists, behind, packed, send):
    del packed
    for who in range(send.shape[0]):
        for turn in range(PAIRS):
            at_first, at_second, is_ahead, _ = places(lists, who, turn)
            send[who, 2 * turn] = behind[at_first]

            @pl.when(jnp.logical_not(is_ahead))
            def _():
                send[who, 2 * turn + 1] = behind[at_second]


def split3(value):
    high = value.astype(BF16)
    low = (value - high.astype(F32)).astype(BF16)
    return high, low


def dot(a, b):
    return jnp.dot(a, b, preferred_element_type=F32)


def fourth(a, b, c, d, sign):
    s_re, s_im, t_re, t_im = a[0] + c[0], a[1] + c[1], a[0] - c[0], a[1] - c[1]
    u_re, u_im, v_re, v_im = b[0] + d[0], b[1] + d[1], b[0] - d[0], b[1] - d[1]
    w_re, w_im = -sign * v_im, sign * v_re
    return (
        (s_re + u_re, s_im + u_im),
        (t_re + w_re, t_im + w_im),
        (s_re - u_re, s_im - u_im),
        (t_re - w_re, t_im - w_im),
    )


def eighth(x, sign):
    low = [(x[k][0] + x[k + 4][0], x[k][1] + x[k + 4][1]) for k in range(4)]
    high = [(x[k][0] - x[k + 4][0], x[k][1] - x[k + 4][1]) for k in range(4)]
    half = np.float32(np.sqrt(0.5))
    turned = [
        high[0],
        (half * (high[1][0] - sign * high[1][1]), half * (high[1][1] + sign * high[1][0])),
        (-sign * high[2][1], sign * high[2][0]),
        (-half * (high[3][0] + sign * high[3][1]), half * (sign * high[3][0] - high[3][1])),
    ]
    even = fourth(*low, sign)
    odd = fourth(*turned, sign)
    return [even[k // 2] if k % 2 == 0 else odd[k // 2] for k in range(SLABS)]


def slab_tiles(re, im):
    count = re.shape[0] // BOX
    return [(re[s * BOX : (s + 1) * BOX], im[s * BOX : (s + 1) * BOX]) for s in range(count)]


def along_x(left3, tiles, sign):
    wide = jnp.concatenate([part for tile in tiles for part in tile], 1)
    high, low = split3(wide)
    both = dot(left3[...], jnp.concatenate([high, low, high], 0))
    re, im = [], []
    for s in range(len(tiles)):
        a, b = slice(2 * s * LANES, (2 * s + 1) * LANES), slice((2 * s + 1) * LANES, (2 * s + 2) * LANES)
        re.append(both[:BOX, a] + sign * both[BOX:, b])
        im.append(both[:BOX, b] - sign * both[BOX:, a])
    return re, im


def right_product(re, im, table):
    high, low = split3(jnp.concatenate([re, im], 1))
    both = dot(jnp.concatenate([high, low, high], 1), table[...])
    return both[:, :LANES], both[:, LANES:]


def by_rows(table):
    return jnp.concatenate(
        [jnp.broadcast_to(table[slab : slab + 1, :], (BOX, LANES)) for slab in range(SLABS)], 0
    )


def poisson(rhos, left3, for3, back3, twid_re, twid_im, green):
    count = len(rhos)
    tiles = [tile for re, im in rhos for tile in eighth(slab_tiles(re, im), -1.0)]
    a_re, a_im = along_x(left3, tiles, -1.0)
    a_re, a_im = jnp.concatenate(a_re, 0), jnp.concatenate(a_im, 0)
    w_re = jnp.concatenate([by_rows(twid_re)] * count, 0)
    w_im = jnp.concatenate([by_rows(twid_im)] * count, 0)
    b_re, b_im = a_re * w_re - a_im * w_im, a_re * w_im + a_im * w_re
    f_re, f_im = right_product(b_re, b_im, for3)
    weight = jnp.concatenate([green[...]] * count, 0)
    c_re, c_im = right_product(f_re * weight, f_im * weight, back3)
    d_re, d_im = c_re * w_re + c_im * w_im, c_im * w_re - c_re * w_im
    e_re, e_im = along_x(left3, slab_tiles(d_re, d_im), 1.0)
    out = []
    for at in range(count):
        picked = slice(at * SLABS, (at + 1) * SLABS)
        tiles = eighth(list(zip(e_re[picked], e_im[picked])), 1.0)
        out.append(tuple(jnp.concatenate([tile[k] for tile in tiles], 0) for k in range(2)))
    return out


def shifted(tile_of, buf, move):
    flat = move[1] * BOX + move[2]
    slabs = flat >> 7
    turn = flat & (LANES - 1)
    for comp in range(2):
        for slab in range(SLABS):
            rolled = pltpu.roll(tile_of(comp, slab), turn, 1)
            buf[comp, PAD_SLABS + slab, PAD_ROWS : PAD_ROWS + BOX, :] = rolled
    lane = lax.broadcasted_iota(jnp.int32, (BOX, LANES), 1)
    row = lax.broadcasted_iota(jnp.int32, (BOX, LANES), 0) - move[0]
    zcell = (lane & (BOX - 1)) - move[2]
    part = (lane >> 5) - move[1]
    base = (row >= 0) & (row < BOX) & (zcell >= 0) & (zcell < BOX)
    straight = lane >= turn
    out = []
    for comp in range(2):
        tiles = []
        for slab in range(SLABS + 1):
            tiles.append(buf[comp, PAD_SLABS - 1 + slab - slabs, pl.ds(PAD_ROWS - move[0], BOX), :])
        parts = []
        for slab in range(SLABS):
            ycell = part + slab * PARTS
            keep = base & (ycell >= 0) & (ycell < BOX)
            picked = jnp.where(straight, tiles[slab + 1], tiles[slab])
            parts.append(jnp.where(keep, picked, 0.0))
        out.append(jnp.concatenate(parts, 0))
    return out


def pair_kernel(
    offsets, lists, got, left3, for3, back3, twid_re, twid_im, green, send, *bufs
):
    members = got.shape[0]
    height = BOX // members
    me = lax.axis_index("grp")

    def field_tile(slot, comp, slab):
        lanes = slice(slab * LANES, (slab + 1) * LANES)
        return jnp.concatenate([got[who, slot, comp, :, lanes] for who in range(members)], 0)

    def field(slot, comp):
        return jnp.concatenate([field_tile(slot, comp, slab) for slab in range(SLABS)], 0)

    def put(slot, comp, value):
        for slab in range(SLABS):
            for who in range(members):
                at = slab * BOX + who * height
                send[who, slot, comp, :, slab * LANES : (slab + 1) * LANES] = value[at : at + height]

    moves, moved, firsts, rhos = [], [], [], []
    for turn in range(PAIRS):
        first = lists[me, 0, turn]
        second = lists[me, 0, PAIRS + turn]
        move = []
        for axis in range(3):
            gap = offsets[axis, second] - offsets[axis, first] + GRID // 2
            gap = jnp.where(gap < 0, gap + GRID, gap)
            gap = jnp.where(gap >= GRID, gap - GRID, gap)
            move.append(gap - GRID // 2)
        moves.append(move)
        m_re, m_im = shifted(
            lambda comp, slab: field_tile(2 * turn + 1, comp, slab), bufs[turn], move
        )
        f_re, f_im = field(2 * turn, 0), field(2 * turn, 1)
        moved.append((m_re, m_im))
        firsts.append((f_re, f_im))
        rhos.append((m_re * f_re + m_im * f_im, m_re * f_im - m_im * f_re))
    pots = poisson(rhos, left3, for3, back3, twid_re, twid_im, green)
    for turn in range(PAIRS):
        (m_re, m_im), (f_re, f_im), (p_re, p_im) = moved[turn], firsts[turn], pots[turn]
        put(2 * turn, 0, m_re * p_re - m_im * p_im)
        put(2 * turn, 1, m_re * p_im + m_im * p_re)
        back = (f_re * p_re + f_im * p_im, f_im * p_re - f_re * p_im)
        s_re, s_im = shifted(
            lambda comp, slab: back[comp][slab * BOX : (slab + 1) * BOX],
            bufs[turn],
            [-step for step in moves[turn]],
        )
        put(2 * turn + 1, 0, s_re)
        put(2 * turn + 1, 1, s_im)


def here_kernel(lists, got, out):
    out[...] = jnp.zeros(out.shape, F32)
    for who in range(got.shape[0]):
        for turn in range(PAIRS):
            _, at_second, is_ahead, _ = places(lists, who, turn)

            @pl.when(is_ahead & (turn < lists[who, 0, 2 * PAIRS]))
            def _():
                out[at_second] -= got[who, 2 * turn + 1]


def back_kernel(lists, got, out):
    out[...] = jnp.zeros(out.shape, F32)
    for who in range(got.shape[0]):
        for turn in range(PAIRS):
            at_first, at_second, is_ahead, differs = places(lists, who, turn)
            live = turn < lists[who, 0, 2 * PAIRS]

            @pl.when(live)
            def _():
                out[at_first] -= got[who, 2 * turn]

            @pl.when(live & differs & jnp.logical_not(is_ahead))
            def _():
                out[at_second] -= got[who, 2 * turn + 1]


def local(orbitals, box_offsets, pair_first, pair_second, pair_count):
    members = lax.axis_size("grp")
    rows = orbitals.shape[2]
    smem = pl.BlockSpec(memory_space=pltpu.SMEM)
    vmem = pl.BlockSpec(memory_space=pltpu.VMEM)
    anywhere = pl.BlockSpec(memory_space=pl.ANY)
    limit = pltpu.CompilerParams(vmem_limit_bytes=40 * 1024 * 1024)
    mine, here = pl.pallas_call(
        entry_kernel,
        out_shape=(
            jax.ShapeDtypeStruct((members, 1, LANES), jnp.int32),
            jax.ShapeDtypeStruct(orbitals.shape, F32),
        ),
        in_specs=[smem] * 3 + [pl.BlockSpec(memory_space=pltpu.HBM)],
        out_specs=(vmem, vmem),
        scratch_shapes=[pltpu.SemaphoreType.DMA],
        compiler_params=limit,
        name="entry",
    )(
        pair_first,
        pair_second,
        pair_count,
        pltpu.with_memory_space_constraint(orbitals, pltpu.HBM),
    )
    mine = from_behind(mine, "orb", 1)
    behind = from_behind(here, "orb", 1)
    lists = lax.psum(mine, "grp")
    slots = 2 * PAIRS
    fields = jax.ShapeDtypeStruct((members, slots, 2, rows, CELLS), F32)
    packed = pl.pallas_call(
        pack_here_kernel,
        out_shape=fields,
        in_specs=[smem, vmem],
        out_specs=vmem,
        compiler_params=limit,
        cost_estimate=pl.CostEstimate(flops=10**10, bytes_accessed=1 << 20, transcendentals=0),
        name="pack_here",
    )(lists, here)
    packed = pl.pallas_call(
        pack_behind_kernel,
        out_shape=fields,
        in_specs=[smem, vmem, vmem],
        out_specs=vmem,
        input_output_aliases={2: 0},
        compiler_params=limit,
        name="pack_behind",
    )(lists, behind, packed)
    got = lax.all_to_all(packed, "grp", 0, 0)
    tables = [jnp.asarray(table) for table in TABLES]
    buf = pltpu.VMEM((2, SLABS + 2 * PAD_SLABS, BOX + 2 * PAD_ROWS, LANES), F32)
    terms = pl.pallas_call(
        pair_kernel,
        out_shape=fields,
        in_specs=[smem] * 2 + [vmem] * 7,
        out_specs=vmem,
        scratch_shapes=[buf] * PAIRS,
        compiler_params=limit,
        name="pairs",
    )(box_offsets, lists, got, *tables)
    returned = lax.all_to_all(terms, "grp", 0, 0)
    shape = jax.ShapeDtypeStruct(orbitals.shape, F32)
    back_terms = pl.pallas_call(
        back_kernel,
        out_shape=shape,
        in_specs=[smem, vmem],
        out_specs=vmem,
        compiler_params=limit,
        name="back_terms",
    )(lists, returned)
    back = from_behind(back_terms, "orb", -1)
    here_terms = pl.pallas_call(
        here_kernel,
        out_shape=shape,
        in_specs=[smem, vmem],
        out_specs=vmem,
        compiler_params=limit,
        name="here_terms",
    )(lists, returned)
    return here_terms + back


def solution(mesh):
    placed = (
        P("orb", None, "grp", None),
        P(),
        P("orb", "grp", None),
        P("orb", "grp", None),
        P("orb", "grp"),
    )
    return jax.shard_map(
        local, mesh=mesh, in_specs=placed, out_specs=P("orb", None, "grp", None), check_vma=False
    )
```

```python
import jax
import jax.numpy as jnp
import ml_dtypes
import numpy as np
from jax import lax
from jax.experimental import pallas as pl
from jax.experimental.pallas import tpu as pltpu
from jax.sharding import PartitionSpec as P

BOX = 32
CELLS = 1024
GRID = 192
ORB_DEV = 6
PAIRS = 2
SCREEN = 0.5
LANES = 128
SLABS = CELLS // LANES
PARTS = LANES // BOX
ROWS = SLABS * BOX
PAD_SLABS = 4
PAD_ROWS = 16
F32 = jnp.float32
BF16 = jnp.bfloat16


def split_bf16(table):
    high = table.astype(ml_dtypes.bfloat16)
    low = (table - high.astype(np.float64)).astype(ml_dtypes.bfloat16)
    return high, low


def make_tables():
    slab, x = np.divmod(np.arange(ROWS), BOX)
    part, z = np.divmod(np.arange(LANES), BOX)
    left = np.exp(-2j * np.pi * np.outer(np.arange(BOX), np.arange(BOX)) / BOX)
    right = np.exp(-2j * np.pi * (np.outer(part, part) / PARTS + np.outer(z, z) / BOX))
    twiddle = np.exp(-2j * np.pi * np.outer(np.arange(SLABS), part) / BOX)
    left_high, left_low = split_bf16(np.concatenate([left.real, left.imag], 0))
    left3 = np.concatenate([left_high, left_high, left_low], 1)
    forward = np.block([[right.real, right.imag], [-right.imag, right.real]])
    for_high, for_low = split_bf16(forward)
    for3 = np.concatenate([for_high, for_high, for_low], 0)
    back_high, back_low = split_bf16(forward.T)
    back3 = np.concatenate([back_high, back_high, back_low], 0)
    lam = (2.0 * np.sin(np.pi * np.arange(BOX) / BOX)) ** 2
    lam_row = lam[x][:, None]
    lam_y = lam[slab[:, None] + SLABS * part[None, :]]
    green = 1.0 / (SCREEN + lam_row + lam_y + lam[z][None, :]) / float(BOX**3)
    return (
        left3,
        for3,
        back3,
        twiddle.real.astype(np.float32),
        twiddle.imag.astype(np.float32),
        green.astype(np.float32),
    )


TABLES = make_tables()


def from_behind(value, axis, steps):
    count = lax.axis_size(axis)
    pairs = [(source, (source + steps) % count) for source in range(count)]
    return lax.ppermute(value, axis, pairs)


def places(lists, who, turn):
    first = lists[who, 0, turn]
    second = lists[who, 0, PAIRS + turn]
    ahead = (first // ORB_DEV) != (second // ORB_DEV)
    return first % ORB_DEV, second % ORB_DEV, ahead, first != second


def entry_kernel(firsts, seconds, count, table):
    who = lax.broadcasted_iota(jnp.int32, table.shape, 0)
    lane = lax.broadcasted_iota(jnp.int32, table.shape, 2)
    value = jnp.where(lane == 2 * PAIRS, count[0, 0], 0)
    for turn in range(PAIRS):
        value = jnp.where(lane == turn, firsts[0, 0, turn], value)
        value = jnp.where(lane == PAIRS + turn, seconds[0, 0, turn], value)
    table[...] = jnp.where(who == lax.axis_index("grp"), value, 0)


def stage_kernel(source, out):
    pltpu.sync_copy(source, out)


def pack_kernel(lists, behind, here, send):
    for who in range(send.shape[0]):
        for turn in range(PAIRS):
            at_first, at_second, is_ahead, _ = places(lists, who, turn)
            send[who, 2 * turn] = behind[at_first]

            @pl.when(is_ahead)
            def _():
                send[who, 2 * turn + 1] = here[at_second]

            @pl.when(jnp.logical_not(is_ahead))
            def _():
                send[who, 2 * turn + 1] = behind[at_second]


def split3(value):
    high = value.astype(BF16)
    low = (value - high.astype(F32)).astype(BF16)
    return high, low


def dot(a, b):
    return jnp.dot(a, b, preferred_element_type=F32)


def fourth(a, b, c, d, sign):
    s_re, s_im, t_re, t_im = a[0] + c[0], a[1] + c[1], a[0] - c[0], a[1] - c[1]
    u_re, u_im, v_re, v_im = b[0] + d[0], b[1] + d[1], b[0] - d[0], b[1] - d[1]
    w_re, w_im = -sign * v_im, sign * v_re
    return (
        (s_re + u_re, s_im + u_im),
        (t_re + w_re, t_im + w_im),
        (s_re - u_re, s_im - u_im),
        (t_re - w_re, t_im - w_im),
    )


def eighth(x, sign):
    low = [(x[k][0] + x[k + 4][0], x[k][1] + x[k + 4][1]) for k in range(4)]
    high = [(x[k][0] - x[k + 4][0], x[k][1] - x[k + 4][1]) for k in range(4)]
    half = np.float32(np.sqrt(0.5))
    turned = [
        high[0],
        (half * (high[1][0] - sign * high[1][1]), half * (high[1][1] + sign * high[1][0])),
        (-sign * high[2][1], sign * high[2][0]),
        (-half * (high[3][0] + sign * high[3][1]), half * (sign * high[3][0] - high[3][1])),
    ]
    even = fourth(*low, sign)
    odd = fourth(*turned, sign)
    return [even[k // 2] if k % 2 == 0 else odd[k // 2] for k in range(SLABS)]


def slab_tiles(re, im):
    count = re.shape[0] // BOX
    return [(re[s * BOX : (s + 1) * BOX], im[s * BOX : (s + 1) * BOX]) for s in range(count)]


def along_x(left3, tiles, sign):
    wide = jnp.concatenate([part for tile in tiles for part in tile], 1)
    high, low = split3(wide)
    both = dot(left3[...], jnp.concatenate([high, low, high], 0))
    re, im = [], []
    for s in range(len(tiles)):
        a, b = slice(2 * s * LANES, (2 * s + 1) * LANES), slice((2 * s + 1) * LANES, (2 * s + 2) * LANES)
        re.append(both[:BOX, a] + sign * both[BOX:, b])
        im.append(both[:BOX, b] - sign * both[BOX:, a])
    return re, im


def right_product(re, im, table):
    high, low = split3(jnp.concatenate([re, im], 1))
    both = dot(jnp.concatenate([high, low, high], 1), table[...])
    return both[:, :LANES], both[:, LANES:]


def by_rows(table):
    return jnp.concatenate(
        [jnp.broadcast_to(table[slab : slab + 1, :], (BOX, LANES)) for slab in range(SLABS)], 0
    )


def poisson(rhos, left3, for3, back3, twid_re, twid_im, green):
    count = len(rhos)
    tiles = [tile for re, im in rhos for tile in eighth(slab_tiles(re, im), -1.0)]
    a_re, a_im = along_x(left3, tiles, -1.0)
    a_re, a_im = jnp.concatenate(a_re, 0), jnp.concatenate(a_im, 0)
    w_re = jnp.concatenate([by_rows(twid_re)] * count, 0)
    w_im = jnp.concatenate([by_rows(twid_im)] * count, 0)
    b_re, b_im = a_re * w_re - a_im * w_im, a_re * w_im + a_im * w_re
    f_re, f_im = right_product(b_re, b_im, for3)
    weight = jnp.concatenate([green[...]] * count, 0)
    c_re, c_im = right_product(f_re * weight, f_im * weight, back3)
    d_re, d_im = c_re * w_re + c_im * w_im, c_im * w_re - c_re * w_im
    e_re, e_im = along_x(left3, slab_tiles(d_re, d_im), 1.0)
    out = []
    for at in range(count):
        picked = slice(at * SLABS, (at + 1) * SLABS)
        tiles = eighth(list(zip(e_re[picked], e_im[picked])), 1.0)
        out.append(tuple(jnp.concatenate([tile[k] for tile in tiles], 0) for k in range(2)))
    return out


def shifted(tile_of, buf, move):
    flat = move[1] * BOX + move[2]
    slabs = flat >> 7
    turn = flat & (LANES - 1)
    for comp in range(2):
        for slab in range(SLABS):
            rolled = pltpu.roll(tile_of(comp, slab), turn, 1)
            buf[comp, PAD_SLABS + slab, PAD_ROWS : PAD_ROWS + BOX, :] = rolled
    lane = lax.broadcasted_iota(jnp.int32, (BOX, LANES), 1)
    row = lax.broadcasted_iota(jnp.int32, (BOX, LANES), 0) - move[0]
    zcell = (lane & (BOX - 1)) - move[2]
    part = (lane >> 5) - move[1]
    base = (row >= 0) & (row < BOX) & (zcell >= 0) & (zcell < BOX)
    straight = lane >= turn
    out = []
    for comp in range(2):
        tiles = []
        for slab in range(SLABS + 1):
            tiles.append(buf[comp, PAD_SLABS - 1 + slab - slabs, pl.ds(PAD_ROWS - move[0], BOX), :])
        parts = []
        for slab in range(SLABS):
            ycell = part + slab * PARTS
            keep = base & (ycell >= 0) & (ycell < BOX)
            picked = jnp.where(straight, tiles[slab + 1], tiles[slab])
            parts.append(jnp.where(keep, picked, 0.0))
        out.append(jnp.concatenate(parts, 0))
    return out


def pair_kernel(
    offsets, lists, got, left3, for3, back3, twid_re, twid_im, green, send, *bufs
):
    members = got.shape[0]
    height = BOX // members
    me = lax.axis_index("grp")

    def field_tile(slot, comp, slab):
        lanes = slice(slab * LANES, (slab + 1) * LANES)
        return jnp.concatenate([got[who, slot, comp, :, lanes] for who in range(members)], 0)

    def field(slot, comp):
        return jnp.concatenate([field_tile(slot, comp, slab) for slab in range(SLABS)], 0)

    def put(slot, comp, value):
        for slab in range(SLABS):
            for who in range(members):
                at = slab * BOX + who * height
                send[who, slot, comp, :, slab * LANES : (slab + 1) * LANES] = value[at : at + height]

    moves, moved, firsts, rhos = [], [], [], []
    for turn in range(PAIRS):
        first = lists[me, 0, turn]
        second = lists[me, 0, PAIRS + turn]
        move = []
        for axis in range(3):
            gap = offsets[axis, second] - offsets[axis, first] + GRID // 2
            gap = jnp.where(gap < 0, gap + GRID, gap)
            gap = jnp.where(gap >= GRID, gap - GRID, gap)
            move.append(gap - GRID // 2)
        moves.append(move)
        m_re, m_im = shifted(
            lambda comp, slab: field_tile(2 * turn + 1, comp, slab), bufs[turn], move
        )
        f_re, f_im = field(2 * turn, 0), field(2 * turn, 1)
        moved.append((m_re, m_im))
        firsts.append((f_re, f_im))
        rhos.append((m_re * f_re + m_im * f_im, m_re * f_im - m_im * f_re))
    pots = poisson(rhos, left3, for3, back3, twid_re, twid_im, green)
    for turn in range(PAIRS):
        (m_re, m_im), (f_re, f_im), (p_re, p_im) = moved[turn], firsts[turn], pots[turn]
        put(2 * turn, 0, m_re * p_re - m_im * p_im)
        put(2 * turn, 1, m_re * p_im + m_im * p_re)
        back = (f_re * p_re + f_im * p_im, f_im * p_re - f_re * p_im)
        s_re, s_im = shifted(
            lambda comp, slab: back[comp][slab * BOX : (slab + 1) * BOX],
            bufs[turn],
            [-step for step in moves[turn]],
        )
        put(2 * turn + 1, 0, s_re)
        put(2 * turn + 1, 1, s_im)


def here_kernel(lists, got, out):
    out[...] = jnp.zeros(out.shape, F32)
    for who in range(got.shape[0]):
        for turn in range(PAIRS):
            _, at_second, is_ahead, _ = places(lists, who, turn)

            @pl.when(is_ahead & (turn < lists[who, 0, 2 * PAIRS]))
            def _():
                out[at_second] -= got[who, 2 * turn + 1]


def back_kernel(lists, got, out):
    out[...] = jnp.zeros(out.shape, F32)
    for who in range(got.shape[0]):
        for turn in range(PAIRS):
            at_first, at_second, is_ahead, differs = places(lists, who, turn)
            live = turn < lists[who, 0, 2 * PAIRS]

            @pl.when(live)
            def _():
                out[at_first] -= got[who, 2 * turn]

            @pl.when(live & differs & jnp.logical_not(is_ahead))
            def _():
                out[at_second] -= got[who, 2 * turn + 1]


def local(orbitals, box_offsets, pair_first, pair_second, pair_count):
    members = lax.axis_size("grp")
    rows = orbitals.shape[2]
    smem = pl.BlockSpec(memory_space=pltpu.SMEM)
    vmem = pl.BlockSpec(memory_space=pltpu.VMEM)
    anywhere = pl.BlockSpec(memory_space=pl.ANY)
    limit = pltpu.CompilerParams(vmem_limit_bytes=40 * 1024 * 1024)
    hbm = pl.BlockSpec(memory_space=pltpu.HBM)
    mine = pl.pallas_call(
        entry_kernel,
        out_shape=jax.ShapeDtypeStruct((members, 1, LANES), jnp.int32),
        in_specs=[smem] * 3,
        out_specs=vmem,
        compiler_params=limit,
        name="entry",
    )(pair_first, pair_second, pair_count)
    mine = from_behind(mine, "orb", 1)
    behind = from_behind(orbitals, "orb", 1)
    lists = lax.psum(mine, "grp")
    slots = 2 * PAIRS
    fields = jax.ShapeDtypeStruct((members, slots, 2, rows, CELLS), F32)
    here = pl.pallas_call(
        stage_kernel,
        out_shape=jax.ShapeDtypeStruct(orbitals.shape, F32),
        in_specs=[hbm],
        out_specs=vmem,
        compiler_params=limit,
        cost_estimate=pl.CostEstimate(flops=10**10, bytes_accessed=1 << 20, transcendentals=0),
        name="stage",
    )(pltpu.with_memory_space_constraint(orbitals, pltpu.HBM))
    packed = pl.pallas_call(
        pack_kernel,
        out_shape=fields,
        in_specs=[smem, vmem, vmem],
        out_specs=vmem,
        compiler_params=limit,
        name="pack",
    )(lists, behind, here)
    got = lax.all_to_all(packed, "grp", 0, 0)
    tables = [jnp.asarray(table) for table in TABLES]
    buf = pltpu.VMEM((2, SLABS + 2 * PAD_SLABS, BOX + 2 * PAD_ROWS, LANES), F32)
    terms = pl.pallas_call(
        pair_kernel,
        out_shape=fields,
        in_specs=[smem] * 2 + [vmem] * 7,
        out_specs=vmem,
        scratch_shapes=[buf] * PAIRS,
        compiler_params=limit,
        name="pairs",
    )(box_offsets, lists, got, *tables)
    returned = lax.all_to_all(terms, "grp", 0, 0)
    shape = jax.ShapeDtypeStruct(orbitals.shape, F32)
    back_terms = pl.pallas_call(
        back_kernel,
        out_shape=shape,
        in_specs=[smem, vmem],
        out_specs=vmem,
        compiler_params=limit,
        name="back_terms",
    )(lists, returned)
    back = from_behind(back_terms, "orb", -1)
    here_terms = pl.pallas_call(
        here_kernel,
        out_shape=shape,
        in_specs=[smem, vmem],
        out_specs=vmem,
        compiler_params=limit,
        name="here_terms",
    )(lists, returned)
    return here_terms + back


def solution(mesh):
    placed = (
        P("orb", None, "grp", None),
        P(),
        P("orb", "grp", None),
        P("orb", "grp", None),
        P("orb", "grp"),
    )
    return jax.shard_map(
        local, mesh=mesh, in_specs=placed, out_specs=P("orb", None, "grp", None), check_vma=False
    )
```

```python
import jax
import jax.numpy as jnp
import ml_dtypes
import numpy as np
from jax import lax
from jax.experimental import pallas as pl
from jax.experimental.pallas import tpu as pltpu
from jax.sharding import PartitionSpec as P

BOX = 32
CELLS = 1024
GRID = 192
ORB_DEV = 6
PAIRS = 2
SCREEN = 0.5
LANES = 128
SLABS = CELLS // LANES
PARTS = LANES // BOX
ROWS = SLABS * BOX
PAD_SLABS = 4
PAD_ROWS = 16
F32 = jnp.float32
BF16 = jnp.bfloat16


def split_bf16(table):
    high = table.astype(ml_dtypes.bfloat16)
    low = (table - high.astype(np.float64)).astype(ml_dtypes.bfloat16)
    return high, low


def make_tables():
    slab, x = np.divmod(np.arange(ROWS), BOX)
    part, z = np.divmod(np.arange(LANES), BOX)
    left = np.exp(-2j * np.pi * np.outer(np.arange(BOX), np.arange(BOX)) / BOX)
    right = np.exp(-2j * np.pi * (np.outer(part, part) / PARTS + np.outer(z, z) / BOX))
    twiddle = np.exp(-2j * np.pi * np.outer(np.arange(SLABS), part) / BOX)
    left_high, left_low = split_bf16(np.concatenate([left.real, left.imag], 0))
    left3 = np.concatenate([left_high, left_high, left_low], 1)
    forward = np.block([[right.real, right.imag], [-right.imag, right.real]])
    for_high, for_low = split_bf16(forward)
    for3 = np.concatenate([for_high, for_high, for_low], 0)
    back_high, back_low = split_bf16(forward.T)
    back3 = np.concatenate([back_high, back_high, back_low], 0)
    lam = (2.0 * np.sin(np.pi * np.arange(BOX) / BOX)) ** 2
    lam_row = lam[x][:, None]
    lam_y = lam[slab[:, None] + SLABS * part[None, :]]
    green = 1.0 / (SCREEN + lam_row + lam_y + lam[z][None, :]) / float(BOX**3)
    return (
        left3,
        for3,
        back3,
        twiddle.real.astype(np.float32),
        twiddle.imag.astype(np.float32),
        green.astype(np.float32),
    )


TABLES = make_tables()


def from_behind(value, axis, steps):
    count = lax.axis_size(axis)
    pairs = [(source, (source + steps) % count) for source in range(count)]
    return lax.ppermute(value, axis, pairs)


def places(lists, who, turn):
    first = lists[who, 0, turn]
    second = lists[who, 0, PAIRS + turn]
    ahead = (first // ORB_DEV) != (second // ORB_DEV)
    return first % ORB_DEV, second % ORB_DEV, ahead, first != second


def entry_kernel(firsts, seconds, count, table):
    who = lax.broadcasted_iota(jnp.int32, table.shape, 0)
    lane = lax.broadcasted_iota(jnp.int32, table.shape, 2)

    def spread(value):
        return jnp.broadcast_to(value.reshape(1, 1, 1), table.shape)

    value = jnp.where(lane == 2 * PAIRS, spread(count[...]), 0)
    for turn in range(PAIRS):
        value = jnp.where(lane == turn, spread(firsts[:, :, turn : turn + 1]), value)
        value = jnp.where(lane == PAIRS + turn, spread(seconds[:, :, turn : turn + 1]), value)
    table[...] = jnp.where(who == lax.axis_index("grp"), value, 0)


def stage_kernel(source, out):
    pltpu.sync_copy(source, out)


def pack_kernel(lists, behind, here, send):
    for who in range(send.shape[0]):
        for turn in range(PAIRS):
            at_first, at_second, is_ahead, _ = places(lists, who, turn)
            send[who, 2 * turn] = behind[at_first]

            @pl.when(is_ahead)
            def _():
                send[who, 2 * turn + 1] = here[at_second]

            @pl.when(jnp.logical_not(is_ahead))
            def _():
                send[who, 2 * turn + 1] = behind[at_second]


def split3(value):
    high = value.astype(BF16)
    low = (value - high.astype(F32)).astype(BF16)
    return high, low


def dot(a, b):
    return jnp.dot(a, b, preferred_element_type=F32)


def fourth(a, b, c, d, sign):
    s_re, s_im, t_re, t_im = a[0] + c[0], a[1] + c[1], a[0] - c[0], a[1] - c[1]
    u_re, u_im, v_re, v_im = b[0] + d[0], b[1] + d[1], b[0] - d[0], b[1] - d[1]
    w_re, w_im = -sign * v_im, sign * v_re
    return (
        (s_re + u_re, s_im + u_im),
        (t_re + w_re, t_im + w_im),
        (s_re - u_re, s_im - u_im),
        (t_re - w_re, t_im - w_im),
    )


def eighth(x, sign):
    low = [(x[k][0] + x[k + 4][0], x[k][1] + x[k + 4][1]) for k in range(4)]
    high = [(x[k][0] - x[k + 4][0], x[k][1] - x[k + 4][1]) for k in range(4)]
    half = np.float32(np.sqrt(0.5))
    turned = [
        high[0],
        (half * (high[1][0] - sign * high[1][1]), half * (high[1][1] + sign * high[1][0])),
        (-sign * high[2][1], sign * high[2][0]),
        (-half * (high[3][0] + sign * high[3][1]), half * (sign * high[3][0] - high[3][1])),
    ]
    even = fourth(*low, sign)
    odd = fourth(*turned, sign)
    return [even[k // 2] if k % 2 == 0 else odd[k // 2] for k in range(SLABS)]


def slab_tiles(re, im):
    count = re.shape[0] // BOX
    return [(re[s * BOX : (s + 1) * BOX], im[s * BOX : (s + 1) * BOX]) for s in range(count)]


def along_x(left3, tiles, sign):
    wide = jnp.concatenate([part for tile in tiles for part in tile], 1)
    high, low = split3(wide)
    both = dot(left3[...], jnp.concatenate([high, low, high], 0))
    re, im = [], []
    for s in range(len(tiles)):
        a, b = slice(2 * s * LANES, (2 * s + 1) * LANES), slice((2 * s + 1) * LANES, (2 * s + 2) * LANES)
        re.append(both[:BOX, a] + sign * both[BOX:, b])
        im.append(both[:BOX, b] - sign * both[BOX:, a])
    return re, im


def right_product(re, im, table):
    high, low = split3(jnp.concatenate([re, im], 1))
    both = dot(jnp.concatenate([high, low, high], 1), table[...])
    return both[:, :LANES], both[:, LANES:]


def by_rows(table):
    return jnp.concatenate(
        [jnp.broadcast_to(table[slab : slab + 1, :], (BOX, LANES)) for slab in range(SLABS)], 0
    )


def poisson(rhos, left3, for3, back3, twid_re, twid_im, green):
    count = len(rhos)
    tiles = [tile for re, im in rhos for tile in eighth(slab_tiles(re, im), -1.0)]
    a_re, a_im = along_x(left3, tiles, -1.0)
    a_re, a_im = jnp.concatenate(a_re, 0), jnp.concatenate(a_im, 0)
    w_re = jnp.concatenate([by_rows(twid_re)] * count, 0)
    w_im = jnp.concatenate([by_rows(twid_im)] * count, 0)
    b_re, b_im = a_re * w_re - a_im * w_im, a_re * w_im + a_im * w_re
    f_re, f_im = right_product(b_re, b_im, for3)
    weight = jnp.concatenate([green[...]] * count, 0)
    c_re, c_im = right_product(f_re * weight, f_im * weight, back3)
    d_re, d_im = c_re * w_re + c_im * w_im, c_im * w_re - c_re * w_im
    e_re, e_im = along_x(left3, slab_tiles(d_re, d_im), 1.0)
    out = []
    for at in range(count):
        picked = slice(at * SLABS, (at + 1) * SLABS)
        tiles = eighth(list(zip(e_re[picked], e_im[picked])), 1.0)
        out.append(tuple(jnp.concatenate([tile[k] for tile in tiles], 0) for k in range(2)))
    return out


def shifted(tile_of, buf, move):
    flat = move[1] * BOX + move[2]
    slabs = flat >> 7
    turn = flat & (LANES - 1)
    for comp in range(2):
        for slab in range(SLABS):
            rolled = pltpu.roll(tile_of(comp, slab), turn, 1)
            buf[comp, PAD_SLABS + slab, PAD_ROWS : PAD_ROWS + BOX, :] = rolled
    lane = lax.broadcasted_iota(jnp.int32, (BOX, LANES), 1)
    row = lax.broadcasted_iota(jnp.int32, (BOX, LANES), 0) - move[0]
    zcell = (lane & (BOX - 1)) - move[2]
    part = (lane >> 5) - move[1]
    base = (row >= 0) & (row < BOX) & (zcell >= 0) & (zcell < BOX)
    straight = lane >= turn
    out = []
    for comp in range(2):
        tiles = []
        for slab in range(SLABS + 1):
            tiles.append(buf[comp, PAD_SLABS - 1 + slab - slabs, pl.ds(PAD_ROWS - move[0], BOX), :])
        parts = []
        for slab in range(SLABS):
            ycell = part + slab * PARTS
            keep = base & (ycell >= 0) & (ycell < BOX)
            picked = jnp.where(straight, tiles[slab + 1], tiles[slab])
            parts.append(jnp.where(keep, picked, 0.0))
        out.append(jnp.concatenate(parts, 0))
    return out


def pair_kernel(
    offsets, lists, got, left3, for3, back3, twid_re, twid_im, green, send, *bufs
):
    members = got.shape[0]
    height = BOX // members
    me = lax.axis_index("grp")

    def field_tile(slot, comp, slab):
        lanes = slice(slab * LANES, (slab + 1) * LANES)
        return jnp.concatenate([got[who, slot, comp, :, lanes] for who in range(members)], 0)

    def field(slot, comp):
        return jnp.concatenate([field_tile(slot, comp, slab) for slab in range(SLABS)], 0)

    def put(slot, comp, value):
        for slab in range(SLABS):
            for who in range(members):
                at = slab * BOX + who * height
                send[who, slot, comp, :, slab * LANES : (slab + 1) * LANES] = value[at : at + height]

    moves, moved, firsts, rhos = [], [], [], []
    for turn in range(PAIRS):
        first = lists[me, 0, turn]
        second = lists[me, 0, PAIRS + turn]
        move = []
        for axis in range(3):
            gap = offsets[axis, second] - offsets[axis, first] + GRID // 2
            gap = jnp.where(gap < 0, gap + GRID, gap)
            gap = jnp.where(gap >= GRID, gap - GRID, gap)
            move.append(gap - GRID // 2)
        moves.append(move)
        m_re, m_im = shifted(
            lambda comp, slab: field_tile(2 * turn + 1, comp, slab), bufs[turn], move
        )
        f_re, f_im = field(2 * turn, 0), field(2 * turn, 1)
        moved.append((m_re, m_im))
        firsts.append((f_re, f_im))
        rhos.append((m_re * f_re + m_im * f_im, m_re * f_im - m_im * f_re))
    pots = poisson(rhos, left3, for3, back3, twid_re, twid_im, green)
    for turn in range(PAIRS):
        (m_re, m_im), (f_re, f_im), (p_re, p_im) = moved[turn], firsts[turn], pots[turn]
        put(2 * turn, 0, m_re * p_re - m_im * p_im)
        put(2 * turn, 1, m_re * p_im + m_im * p_re)
        back = (f_re * p_re + f_im * p_im, f_im * p_re - f_re * p_im)
        s_re, s_im = shifted(
            lambda comp, slab: back[comp][slab * BOX : (slab + 1) * BOX],
            bufs[turn],
            [-step for step in moves[turn]],
        )
        put(2 * turn + 1, 0, s_re)
        put(2 * turn + 1, 1, s_im)


def here_kernel(lists, got, out):
    out[...] = jnp.zeros(out.shape, F32)
    for who in range(got.shape[0]):
        for turn in range(PAIRS):
            _, at_second, is_ahead, _ = places(lists, who, turn)

            @pl.when(is_ahead & (turn < lists[who, 0, 2 * PAIRS]))
            def _():
                out[at_second] -= got[who, 2 * turn + 1]


def back_kernel(lists, got, out):
    out[...] = jnp.zeros(out.shape, F32)
    for who in range(got.shape[0]):
        for turn in range(PAIRS):
            at_first, at_second, is_ahead, differs = places(lists, who, turn)
            live = turn < lists[who, 0, 2 * PAIRS]

            @pl.when(live)
            def _():
                out[at_first] -= got[who, 2 * turn]

            @pl.when(live & differs & jnp.logical_not(is_ahead))
            def _():
                out[at_second] -= got[who, 2 * turn + 1]


def local(orbitals, box_offsets, pair_first, pair_second, pair_count):
    members = lax.axis_size("grp")
    rows = orbitals.shape[2]
    smem = pl.BlockSpec(memory_space=pltpu.SMEM)
    vmem = pl.BlockSpec(memory_space=pltpu.VMEM)
    anywhere = pl.BlockSpec(memory_space=pl.ANY)
    limit = pltpu.CompilerParams(vmem_limit_bytes=40 * 1024 * 1024)
    hbm = pl.BlockSpec(memory_space=pltpu.HBM)
    mine = pl.pallas_call(
        entry_kernel,
        out_shape=jax.ShapeDtypeStruct((members, 1, LANES), jnp.int32),
        in_specs=[vmem] * 3,
        out_specs=vmem,
        compiler_params=limit,
        name="entry",
    )(pair_first, pair_second, pair_count)
    mine = from_behind(mine, "orb", 1)
    behind = from_behind(orbitals, "orb", 1)
    lists = lax.psum(mine, "grp")
    slots = 2 * PAIRS
    fields = jax.ShapeDtypeStruct((members, slots, 2, rows, CELLS), F32)
    here = pl.pallas_call(
        stage_kernel,
        out_shape=jax.ShapeDtypeStruct(orbitals.shape, F32),
        in_specs=[hbm],
        out_specs=vmem,
        compiler_params=limit,
        cost_estimate=pl.CostEstimate(flops=10**10, bytes_accessed=1 << 20, transcendentals=0),
        name="stage",
    )(pltpu.with_memory_space_constraint(orbitals, pltpu.HBM))
    packed = pl.pallas_call(
        pack_kernel,
        out_shape=fields,
        in_specs=[smem, vmem, vmem],
        out_specs=vmem,
        compiler_params=limit,
        name="pack",
    )(lists, behind, here)
    got = lax.all_to_all(packed, "grp", 0, 0)
    tables = [jnp.asarray(table) for table in TABLES]
    buf = pltpu.VMEM((2, SLABS + 2 * PAD_SLABS, BOX + 2 * PAD_ROWS, LANES), F32)
    terms = pl.pallas_call(
        pair_kernel,
        out_shape=fields,
        in_specs=[smem] * 2 + [vmem] * 7,
        out_specs=vmem,
        scratch_shapes=[buf] * PAIRS,
        compiler_params=limit,
        name="pairs",
    )(box_offsets, lists, got, *tables)
    returned = lax.all_to_all(terms, "grp", 0, 0)
    shape = jax.ShapeDtypeStruct(orbitals.shape, F32)
    back_terms = pl.pallas_call(
        back_kernel,
        out_shape=shape,
        in_specs=[smem, vmem],
        out_specs=vmem,
        compiler_params=limit,
        name="back_terms",
    )(lists, returned)
    back = from_behind(back_terms, "orb", -1)
    here_terms = pl.pallas_call(
        here_kernel,
        out_shape=shape,
        in_specs=[smem, vmem],
        out_specs=vmem,
        compiler_params=limit,
        name="here_terms",
    )(lists, returned)
    return here_terms + back


def solution(mesh):
    placed = (
        P("orb", None, "grp", None),
        P(),
        P("orb", "grp", None),
        P("orb", "grp", None),
        P("orb", "grp"),
    )
    return jax.shard_map(
        local, mesh=mesh, in_specs=placed, out_specs=P("orb", None, "grp", None), check_vma=False
    )
```

```python
import jax
import jax.numpy as jnp
import ml_dtypes
import numpy as np
from jax import lax
from jax.experimental import pallas as pl
from jax.experimental.pallas import tpu as pltpu
from jax.sharding import PartitionSpec as P

BOX = 32
CELLS = 1024
GRID = 192
ORB_DEV = 6
PAIRS = 2
SCREEN = 0.5
LANES = 128
SLABS = CELLS // LANES
PARTS = LANES // BOX
ROWS = SLABS * BOX
PAD_SLABS = 4
PAD_ROWS = 16
F32 = jnp.float32
BF16 = jnp.bfloat16


def split_bf16(table):
    high = table.astype(ml_dtypes.bfloat16)
    low = (table - high.astype(np.float64)).astype(ml_dtypes.bfloat16)
    return high, low


def make_tables():
    slab, x = np.divmod(np.arange(ROWS), BOX)
    part, z = np.divmod(np.arange(LANES), BOX)
    left = np.exp(-2j * np.pi * np.outer(np.arange(BOX), np.arange(BOX)) / BOX)
    right = np.exp(-2j * np.pi * (np.outer(part, part) / PARTS + np.outer(z, z) / BOX))
    twiddle = np.exp(-2j * np.pi * np.outer(np.arange(SLABS), part) / BOX)
    left_high, left_low = split_bf16(np.concatenate([left.real, left.imag], 0))
    left3 = np.concatenate([left_high, left_high, left_low], 1)
    forward = np.block([[right.real, right.imag], [-right.imag, right.real]])
    for_high, for_low = split_bf16(forward)
    for3 = np.concatenate([for_high, for_high, for_low], 0)
    back_high, back_low = split_bf16(forward.T)
    back3 = np.concatenate([back_high, back_high, back_low], 0)
    lam = (2.0 * np.sin(np.pi * np.arange(BOX) / BOX)) ** 2
    lam_row = lam[x][:, None]
    lam_y = lam[slab[:, None] + SLABS * part[None, :]]
    green = 1.0 / (SCREEN + lam_row + lam_y + lam[z][None, :]) / float(BOX**3)
    return (
        left3,
        for3,
        back3,
        twiddle.real.astype(np.float32),
        twiddle.imag.astype(np.float32),
        green.astype(np.float32),
    )


TABLES = make_tables()


def from_behind(value, axis, steps):
    count = lax.axis_size(axis)
    pairs = [(source, (source + steps) % count) for source in range(count)]
    return lax.ppermute(value, axis, pairs)


def entry_kernel(firsts, seconds, count, table):
    who = lax.broadcasted_iota(jnp.int32, table.shape, 0)
    lane = lax.broadcasted_iota(jnp.int32, table.shape, 2)

    def spread(value):
        return jnp.broadcast_to(value.reshape(1, 1, 1), table.shape)

    def block_of(orbital):
        return (orbital * 10923) >> 16

    live = spread(count[...])
    row = jnp.zeros(table.shape, jnp.int32)
    for turn in range(PAIRS):
        first = spread(firsts[:, :, turn : turn + 1])
        second = spread(seconds[:, :, turn : turn + 1])
        first_block, second_block = block_of(first), block_of(second)
        code = (first - first_block * ORB_DEV) | ((second - second_block * ORB_DEV) << 3)
        code |= jnp.where(first_block != second_block, 64, 0)
        code |= jnp.where(first != second, 128, 0)
        code |= jnp.where(turn < live, 256, 0)
        row = jnp.where(lane == 3 * turn, first, row)
        row = jnp.where(lane == 3 * turn + 1, second, row)
        row = jnp.where(lane == 3 * turn + 2, code, row)
    table[...] = jnp.where(who == lax.axis_index("grp"), row, 0)


def places(lists, who, turn):
    code = lists[who, 0, 3 * turn + 2]
    return code & 7, (code >> 3) & 7, (code & 64) != 0, (code & 128) != 0, (code & 256) != 0


def stage_kernel(source, out):
    pltpu.sync_copy(source, out)


def pack_kernel(lists, behind, here, send):
    for who in range(send.shape[0]):
        for turn in range(PAIRS):
            at_first, at_second, is_ahead, _, _ = places(lists, who, turn)
            send[who, 2 * turn] = behind[at_first]

            @pl.when(is_ahead)
            def _():
                send[who, 2 * turn + 1] = here[at_second]

            @pl.when(jnp.logical_not(is_ahead))
            def _():
                send[who, 2 * turn + 1] = behind[at_second]


def split3(value):
    high = value.astype(BF16)
    low = (value - high.astype(F32)).astype(BF16)
    return high, low


def dot(a, b):
    return jnp.dot(a, b, preferred_element_type=F32)


def fourth(a, b, c, d, sign):
    s_re, s_im, t_re, t_im = a[0] + c[0], a[1] + c[1], a[0] - c[0], a[1] - c[1]
    u_re, u_im, v_re, v_im = b[0] + d[0], b[1] + d[1], b[0] - d[0], b[1] - d[1]
    w_re, w_im = -sign * v_im, sign * v_re
    return (
        (s_re + u_re, s_im + u_im),
        (t_re + w_re, t_im + w_im),
        (s_re - u_re, s_im - u_im),
        (t_re - w_re, t_im - w_im),
    )


def eighth(x, sign):
    low = [(x[k][0] + x[k + 4][0], x[k][1] + x[k + 4][1]) for k in range(4)]
    high = [(x[k][0] - x[k + 4][0], x[k][1] - x[k + 4][1]) for k in range(4)]
    half = np.float32(np.sqrt(0.5))
    turned = [
        high[0],
        (half * (high[1][0] - sign * high[1][1]), half * (high[1][1] + sign * high[1][0])),
        (-sign * high[2][1], sign * high[2][0]),
        (-half * (high[3][0] + sign * high[3][1]), half * (sign * high[3][0] - high[3][1])),
    ]
    even = fourth(*low, sign)
    odd = fourth(*turned, sign)
    return [even[k // 2] if k % 2 == 0 else odd[k // 2] for k in range(SLABS)]


def slab_tiles(re, im):
    count = re.shape[0] // BOX
    return [(re[s * BOX : (s + 1) * BOX], im[s * BOX : (s + 1) * BOX]) for s in range(count)]


def along_x(left3, tiles, sign):
    wide = jnp.concatenate([part for tile in tiles for part in tile], 1)
    high, low = split3(wide)
    both = dot(left3[...], jnp.concatenate([high, low, high], 0))
    re, im = [], []
    for s in range(len(tiles)):
        a, b = slice(2 * s * LANES, (2 * s + 1) * LANES), slice((2 * s + 1) * LANES, (2 * s + 2) * LANES)
        re.append(both[:BOX, a] + sign * both[BOX:, b])
        im.append(both[:BOX, b] - sign * both[BOX:, a])
    return re, im


def right_product(re, im, table):
    high, low = split3(jnp.concatenate([re, im], 1))
    both = dot(jnp.concatenate([high, low, high], 1), table[...])
    return both[:, :LANES], both[:, LANES:]


def by_rows(table):
    return jnp.concatenate(
        [jnp.broadcast_to(table[slab : slab + 1, :], (BOX, LANES)) for slab in range(SLABS)], 0
    )


def poisson(rhos, left3, for3, back3, twid_re, twid_im, green):
    count = len(rhos)
    tiles = [tile for re, im in rhos for tile in eighth(slab_tiles(re, im), -1.0)]
    a_re, a_im = along_x(left3, tiles, -1.0)
    a_re, a_im = jnp.concatenate(a_re, 0), jnp.concatenate(a_im, 0)
    w_re = jnp.concatenate([by_rows(twid_re)] * count, 0)
    w_im = jnp.concatenate([by_rows(twid_im)] * count, 0)
    b_re, b_im = a_re * w_re - a_im * w_im, a_re * w_im + a_im * w_re
    f_re, f_im = right_product(b_re, b_im, for3)
    weight = jnp.concatenate([green[...]] * count, 0)
    c_re, c_im = right_product(f_re * weight, f_im * weight, back3)
    d_re, d_im = c_re * w_re + c_im * w_im, c_im * w_re - c_re * w_im
    e_re, e_im = along_x(left3, slab_tiles(d_re, d_im), 1.0)
    out = []
    for at in range(count):
        picked = slice(at * SLABS, (at + 1) * SLABS)
        tiles = eighth(list(zip(e_re[picked], e_im[picked])), 1.0)
        out.append(tuple(jnp.concatenate([tile[k] for tile in tiles], 0) for k in range(2)))
    return out


def shifted(tile_of, buf, move):
    flat = move[1] * BOX + move[2]
    slabs = flat >> 7
    turn = flat & (LANES - 1)
    for comp in range(2):
        for slab in range(SLABS):
            rolled = pltpu.roll(tile_of(comp, slab), turn, 1)
            buf[comp, PAD_SLABS + slab, PAD_ROWS : PAD_ROWS + BOX, :] = rolled
    lane = lax.broadcasted_iota(jnp.int32, (BOX, LANES), 1)
    row = lax.broadcasted_iota(jnp.int32, (BOX, LANES), 0) - move[0]
    zcell = (lane & (BOX - 1)) - move[2]
    part = (lane >> 5) - move[1]
    base = (row >= 0) & (row < BOX) & (zcell >= 0) & (zcell < BOX)
    straight = lane >= turn
    out = []
    for comp in range(2):
        tiles = []
        for slab in range(SLABS + 1):
            tiles.append(buf[comp, PAD_SLABS - 1 + slab - slabs, pl.ds(PAD_ROWS - move[0], BOX), :])
        parts = []
        for slab in range(SLABS):
            ycell = part + slab * PARTS
            keep = base & (ycell >= 0) & (ycell < BOX)
            picked = jnp.where(straight, tiles[slab + 1], tiles[slab])
            parts.append(jnp.where(keep, picked, 0.0))
        out.append(jnp.concatenate(parts, 0))
    return out


def pair_kernel(
    offsets, lists, got, left3, for3, back3, twid_re, twid_im, green, send, *bufs
):
    members = got.shape[0]
    height = BOX // members
    me = lax.axis_index("grp")

    def field_tile(slot, comp, slab):
        lanes = slice(slab * LANES, (slab + 1) * LANES)
        return jnp.concatenate([got[who, slot, comp, :, lanes] for who in range(members)], 0)

    def field(slot, comp):
        return jnp.concatenate([field_tile(slot, comp, slab) for slab in range(SLABS)], 0)

    def put(slot, comp, value):
        for slab in range(SLABS):
            for who in range(members):
                at = slab * BOX + who * height
                send[who, slot, comp, :, slab * LANES : (slab + 1) * LANES] = value[at : at + height]

    moves, moved, firsts, rhos = [], [], [], []
    for turn in range(PAIRS):
        first = lists[me, 0, 3 * turn]
        second = lists[me, 0, 3 * turn + 1]
        move = []
        for axis in range(3):
            gap = offsets[axis, second] - offsets[axis, first] + GRID // 2
            gap = jnp.where(gap < 0, gap + GRID, gap)
            gap = jnp.where(gap >= GRID, gap - GRID, gap)
            move.append(gap - GRID // 2)
        moves.append(move)
        m_re, m_im = shifted(
            lambda comp, slab: field_tile(2 * turn + 1, comp, slab), bufs[turn], move
        )
        f_re, f_im = field(2 * turn, 0), field(2 * turn, 1)
        moved.append((m_re, m_im))
        firsts.append((f_re, f_im))
        rhos.append((m_re * f_re + m_im * f_im, m_re * f_im - m_im * f_re))
    pots = poisson(rhos, left3, for3, back3, twid_re, twid_im, green)
    for turn in range(PAIRS):
        (m_re, m_im), (f_re, f_im), (p_re, p_im) = moved[turn], firsts[turn], pots[turn]
        put(2 * turn, 0, m_re * p_re - m_im * p_im)
        put(2 * turn, 1, m_re * p_im + m_im * p_re)
        back = (f_re * p_re + f_im * p_im, f_im * p_re - f_re * p_im)
        s_re, s_im = shifted(
            lambda comp, slab: back[comp][slab * BOX : (slab + 1) * BOX],
            bufs[turn],
            [-step for step in moves[turn]],
        )
        put(2 * turn + 1, 0, s_re)
        put(2 * turn + 1, 1, s_im)


def here_kernel(lists, got, out):
    out[...] = jnp.zeros(out.shape, F32)
    for who in range(got.shape[0]):
        for turn in range(PAIRS):
            _, at_second, is_ahead, _, live = places(lists, who, turn)

            @pl.when(is_ahead & live)
            def _():
                out[at_second] -= got[who, 2 * turn + 1]


def back_kernel(lists, got, out):
    out[...] = jnp.zeros(out.shape, F32)
    for who in range(got.shape[0]):
        for turn in range(PAIRS):
            at_first, at_second, is_ahead, differs, live = places(lists, who, turn)

            @pl.when(live)
            def _():
                out[at_first] -= got[who, 2 * turn]

            @pl.when(live & differs & jnp.logical_not(is_ahead))
            def _():
                out[at_second] -= got[who, 2 * turn + 1]


def local(orbitals, box_offsets, pair_first, pair_second, pair_count):
    members = lax.axis_size("grp")
    rows = orbitals.shape[2]
    smem = pl.BlockSpec(memory_space=pltpu.SMEM)
    vmem = pl.BlockSpec(memory_space=pltpu.VMEM)
    anywhere = pl.BlockSpec(memory_space=pl.ANY)
    limit = pltpu.CompilerParams(vmem_limit_bytes=40 * 1024 * 1024)
    hbm = pl.BlockSpec(memory_space=pltpu.HBM)
    mine = pl.pallas_call(
        entry_kernel,
        out_shape=jax.ShapeDtypeStruct((members, 1, LANES), jnp.int32),
        in_specs=[vmem] * 3,
        out_specs=vmem,
        compiler_params=limit,
        name="entry",
    )(pair_first, pair_second, pair_count)
    mine = from_behind(mine, "orb", 1)
    behind = from_behind(orbitals, "orb", 1)
    lists = lax.psum(mine, "grp")
    slots = 2 * PAIRS
    fields = jax.ShapeDtypeStruct((members, slots, 2, rows, CELLS), F32)
    here = pl.pallas_call(
        stage_kernel,
        out_shape=jax.ShapeDtypeStruct(orbitals.shape, F32),
        in_specs=[hbm],
        out_specs=vmem,
        compiler_params=limit,
        cost_estimate=pl.CostEstimate(flops=10**10, bytes_accessed=1 << 20, transcendentals=0),
        name="stage",
    )(pltpu.with_memory_space_constraint(orbitals, pltpu.HBM))
    packed = pl.pallas_call(
        pack_kernel,
        out_shape=fields,
        in_specs=[smem, vmem, vmem],
        out_specs=vmem,
        compiler_params=limit,
        name="pack",
    )(lists, behind, here)
    got = lax.all_to_all(packed, "grp", 0, 0)
    tables = [jnp.asarray(table) for table in TABLES]
    buf = pltpu.VMEM((2, SLABS + 2 * PAD_SLABS, BOX + 2 * PAD_ROWS, LANES), F32)
    terms = pl.pallas_call(
        pair_kernel,
        out_shape=fields,
        in_specs=[smem] * 2 + [vmem] * 7,
        out_specs=vmem,
        scratch_shapes=[buf] * PAIRS,
        compiler_params=limit,
        name="pairs",
    )(box_offsets, lists, got, *tables)
    returned = lax.all_to_all(terms, "grp", 0, 0)
    shape = jax.ShapeDtypeStruct(orbitals.shape, F32)
    back_terms = pl.pallas_call(
        back_kernel,
        out_shape=shape,
        in_specs=[smem, vmem],
        out_specs=vmem,
        compiler_params=limit,
        name="back_terms",
    )(lists, returned)
    back = from_behind(back_terms, "orb", -1)
    here_terms = pl.pallas_call(
        here_kernel,
        out_shape=shape,
        in_specs=[smem, vmem],
        out_specs=vmem,
        compiler_params=limit,
        name="here_terms",
    )(lists, returned)
    return here_terms + back


def solution(mesh):
    placed = (
        P("orb", None, "grp", None),
        P(),
        P("orb", "grp", None),
        P("orb", "grp", None),
        P("orb", "grp"),
    )
    return jax.shard_map(
        local, mesh=mesh, in_specs=placed, out_specs=P("orb", None, "grp", None), check_vma=False
    )
```

```python
import jax
import jax.numpy as jnp
import ml_dtypes
import numpy as np
from jax import lax
from jax.experimental import pallas as pl
from jax.experimental.pallas import tpu as pltpu
from jax.sharding import PartitionSpec as P

BOX = 32
CELLS = 1024
GRID = 192
ORB_DEV = 6
PAIRS = 2
SCREEN = 0.5
LANES = 128
SLABS = CELLS // LANES
PARTS = LANES // BOX
ROWS = SLABS * BOX
PAD_SLABS = 4
PAD_ROWS = 16
F32 = jnp.float32
BF16 = jnp.bfloat16


def split_bf16(table):
    high = table.astype(ml_dtypes.bfloat16)
    low = (table - high.astype(np.float64)).astype(ml_dtypes.bfloat16)
    return high, low


def make_tables():
    slab, x = np.divmod(np.arange(ROWS), BOX)
    part, z = np.divmod(np.arange(LANES), BOX)
    left = np.exp(-2j * np.pi * np.outer(np.arange(BOX), np.arange(BOX)) / BOX)
    right = np.exp(-2j * np.pi * (np.outer(part, part) / PARTS + np.outer(z, z) / BOX))
    twiddle = np.exp(-2j * np.pi * np.outer(np.arange(SLABS), part) / BOX)
    left_high, left_low = split_bf16(np.concatenate([left.real, left.imag], 0))
    left3 = np.concatenate([left_high, left_high, left_low], 1)
    forward = np.block([[right.real, right.imag], [-right.imag, right.real]])
    for_high, for_low = split_bf16(forward)
    for3 = np.concatenate([for_high, for_high, for_low], 0)
    back_high, back_low = split_bf16(forward.T)
    back3 = np.concatenate([back_high, back_high, back_low], 0)
    lam = (2.0 * np.sin(np.pi * np.arange(BOX) / BOX)) ** 2
    lam_row = lam[x][:, None]
    lam_y = lam[slab[:, None] + SLABS * part[None, :]]
    green = 1.0 / (SCREEN + lam_row + lam_y + lam[z][None, :]) / float(BOX**3)
    return (
        left3,
        for3,
        back3,
        twiddle.real.astype(np.float32),
        twiddle.imag.astype(np.float32),
        green.astype(np.float32),
    )


TABLES = make_tables()


def from_behind(value, axis, steps):
    count = lax.axis_size(axis)
    pairs = [(source, (source + steps) % count) for source in range(count)]
    return lax.ppermute(value, axis, pairs)


def entry_kernel(firsts, seconds, count, table):
    who = lax.broadcasted_iota(jnp.int32, table.shape, 0)
    lane = lax.broadcasted_iota(jnp.int32, table.shape, 2)

    def spread(value):
        return jnp.broadcast_to(value.reshape(1, 1, 1), table.shape)

    def block_of(orbital):
        return (orbital * 10923) >> 16

    live = spread(count[...])
    row = jnp.zeros(table.shape, jnp.int32)
    for turn in range(PAIRS):
        first = spread(firsts[:, :, turn : turn + 1])
        second = spread(seconds[:, :, turn : turn + 1])
        first_block, second_block = block_of(first), block_of(second)
        code = (first - first_block * ORB_DEV) | ((second - second_block * ORB_DEV) << 3)
        code |= jnp.where(first_block != second_block, 64, 0)
        code |= jnp.where(first != second, 128, 0)
        code |= jnp.where(turn < live, 256, 0)
        row = jnp.where(lane == 3 * turn, first, row)
        row = jnp.where(lane == 3 * turn + 1, second, row)
        row = jnp.where(lane == 3 * turn + 2, code, row)
    table[...] = jnp.where(who == lax.axis_index("grp"), row, 0)


def places(lists, who, turn):
    code = lists[who, 0, 3 * turn + 2]
    return code & 7, (code >> 3) & 7, (code & 64) != 0, (code & 128) != 0, (code & 256) != 0


def stage_kernel(source, out):
    pltpu.sync_copy(source, out)


def pack_kernel(lists, behind, here, send):
    for who in range(send.shape[0]):
        for turn in range(PAIRS):
            at_first, at_second, is_ahead, _, _ = places(lists, who, turn)
            send[who, 2 * turn] = behind[at_first]

            @pl.when(is_ahead)
            def _():
                send[who, 2 * turn + 1] = here[at_second]

            @pl.when(jnp.logical_not(is_ahead))
            def _():
                send[who, 2 * turn + 1] = behind[at_second]


def split3(value):
    high = value.astype(BF16)
    low = (value - high.astype(F32)).astype(BF16)
    return high, low


def dot(a, b):
    return jnp.dot(a, b, preferred_element_type=F32)


def fourth(a, b, c, d, sign):
    s_re, s_im, t_re, t_im = a[0] + c[0], a[1] + c[1], a[0] - c[0], a[1] - c[1]
    u_re, u_im, v_re, v_im = b[0] + d[0], b[1] + d[1], b[0] - d[0], b[1] - d[1]
    w_re, w_im = -sign * v_im, sign * v_re
    return (
        (s_re + u_re, s_im + u_im),
        (t_re + w_re, t_im + w_im),
        (s_re - u_re, s_im - u_im),
        (t_re - w_re, t_im - w_im),
    )


def eighth(x, sign):
    low = [(x[k][0] + x[k + 4][0], x[k][1] + x[k + 4][1]) for k in range(4)]
    high = [(x[k][0] - x[k + 4][0], x[k][1] - x[k + 4][1]) for k in range(4)]
    half = np.float32(np.sqrt(0.5))
    turned = [
        high[0],
        (half * (high[1][0] - sign * high[1][1]), half * (high[1][1] + sign * high[1][0])),
        (-sign * high[2][1], sign * high[2][0]),
        (-half * (high[3][0] + sign * high[3][1]), half * (sign * high[3][0] - high[3][1])),
    ]
    even = fourth(*low, sign)
    odd = fourth(*turned, sign)
    return [even[k // 2] if k % 2 == 0 else odd[k // 2] for k in range(SLABS)]


def slab_tiles(re, im):
    count = re.shape[0] // BOX
    return [(re[s * BOX : (s + 1) * BOX], im[s * BOX : (s + 1) * BOX]) for s in range(count)]


def along_x(left3, tiles, sign):
    wide = jnp.concatenate([part for tile in tiles for part in tile], 1)
    high, low = split3(wide)
    both = dot(left3[...], jnp.concatenate([high, low, high], 0))
    re, im = [], []
    for s in range(len(tiles)):
        a, b = slice(2 * s * LANES, (2 * s + 1) * LANES), slice((2 * s + 1) * LANES, (2 * s + 2) * LANES)
        re.append(both[:BOX, a] + sign * both[BOX:, b])
        im.append(both[:BOX, b] - sign * both[BOX:, a])
    return re, im


def right_product(re, im, table):
    high, low = split3(jnp.concatenate([re, im], 1))
    both = dot(jnp.concatenate([high, low, high], 1), table[...])
    return both[:, :LANES], both[:, LANES:]


def by_rows(table):
    return jnp.concatenate(
        [jnp.broadcast_to(table[slab : slab + 1, :], (BOX, LANES)) for slab in range(SLABS)], 0
    )


def poisson(rhos, left3, for3, back3, twid_re, twid_im, green):
    count = len(rhos)
    tiles = [tile for re, im in rhos for tile in eighth(slab_tiles(re, im), -1.0)]
    a_re, a_im = along_x(left3, tiles, -1.0)
    a_re, a_im = jnp.concatenate(a_re, 0), jnp.concatenate(a_im, 0)
    w_re = jnp.concatenate([by_rows(twid_re)] * count, 0)
    w_im = jnp.concatenate([by_rows(twid_im)] * count, 0)
    b_re, b_im = a_re * w_re - a_im * w_im, a_re * w_im + a_im * w_re
    f_re, f_im = right_product(b_re, b_im, for3)
    weight = jnp.concatenate([green[...]] * count, 0)
    c_re, c_im = right_product(f_re * weight, f_im * weight, back3)
    d_re, d_im = c_re * w_re + c_im * w_im, c_im * w_re - c_re * w_im
    e_re, e_im = along_x(left3, slab_tiles(d_re, d_im), 1.0)
    out = []
    for at in range(count):
        picked = slice(at * SLABS, (at + 1) * SLABS)
        tiles = eighth(list(zip(e_re[picked], e_im[picked])), 1.0)
        out.append(tuple(jnp.concatenate([tile[k] for tile in tiles], 0) for k in range(2)))
    return out


def shifted(tile_of, buf, move):
    flat = move[1] * BOX + move[2]
    slabs = flat >> 7
    turn = flat & (LANES - 1)
    for comp in range(2):
        for slab in range(SLABS):
            rolled = pltpu.roll(tile_of(comp, slab), turn, 1)
            buf[comp, PAD_SLABS + slab, PAD_ROWS : PAD_ROWS + BOX, :] = rolled
    lane = lax.broadcasted_iota(jnp.int32, (BOX, LANES), 1)
    row = lax.broadcasted_iota(jnp.int32, (BOX, LANES), 0) - move[0]
    zcell = (lane & (BOX - 1)) - move[2]
    part = (lane >> 5) - move[1]
    base = (row >= 0) & (row < BOX) & (zcell >= 0) & (zcell < BOX)
    straight = lane >= turn
    out = []
    for comp in range(2):
        tiles = []
        for slab in range(SLABS + 1):
            tiles.append(buf[comp, PAD_SLABS - 1 + slab - slabs, pl.ds(PAD_ROWS - move[0], BOX), :])
        parts = []
        for slab in range(SLABS):
            ycell = part + slab * PARTS
            keep = base & (ycell >= 0) & (ycell < BOX)
            picked = jnp.where(straight, tiles[slab + 1], tiles[slab])
            parts.append(jnp.where(keep, picked, 0.0))
        out.append(jnp.concatenate(parts, 0))
    return out


def pair_kernel(
    offsets, lists, got, left3, for3, back3, twid_re, twid_im, green, send, *bufs
):
    members = got.shape[0]
    height = BOX // members
    me = lax.axis_index("grp")

    def field_tile(slot, comp, slab):
        lanes = slice(slab * LANES, (slab + 1) * LANES)
        return jnp.concatenate([got[who, slot, comp, :, lanes] for who in range(members)], 0)

    def field(slot, comp):
        return jnp.concatenate([field_tile(slot, comp, slab) for slab in range(SLABS)], 0)

    def put(slot, comp, value):
        for slab in range(SLABS):
            for who in range(members):
                at = slab * BOX + who * height
                send[who, slot, comp, :, slab * LANES : (slab + 1) * LANES] = value[at : at + height]

    moves, moved, firsts, rhos = [], [], [], []
    for turn in range(PAIRS):
        first = lists[me, 0, 3 * turn]
        second = lists[me, 0, 3 * turn + 1]
        move = []
        for axis in range(3):
            gap = offsets[axis, second] - offsets[axis, first] + GRID // 2
            gap = jnp.where(gap < 0, gap + GRID, gap)
            gap = jnp.where(gap >= GRID, gap - GRID, gap)
            move.append(gap - GRID // 2)
        moves.append(move)
        m_re, m_im = shifted(
            lambda comp, slab: field_tile(2 * turn + 1, comp, slab), bufs[turn], move
        )
        f_re, f_im = field(2 * turn, 0), field(2 * turn, 1)
        moved.append((m_re, m_im))
        firsts.append((f_re, f_im))
        rhos.append((m_re * f_re + m_im * f_im, m_re * f_im - m_im * f_re))
    pots = poisson(rhos, left3, for3, back3, twid_re, twid_im, green)
    for turn in range(PAIRS):
        (m_re, m_im), (f_re, f_im), (p_re, p_im) = moved[turn], firsts[turn], pots[turn]
        put(2 * turn, 0, m_re * p_re - m_im * p_im)
        put(2 * turn, 1, m_re * p_im + m_im * p_re)
        back = (f_re * p_re + f_im * p_im, f_im * p_re - f_re * p_im)
        s_re, s_im = shifted(
            lambda comp, slab: back[comp][slab * BOX : (slab + 1) * BOX],
            bufs[turn],
            [-step for step in moves[turn]],
        )
        put(2 * turn + 1, 0, s_re)
        put(2 * turn + 1, 1, s_im)


def here_kernel(lists, got, out):
    out[...] = jnp.zeros(out.shape, F32)
    for who in range(got.shape[0]):
        for turn in range(PAIRS):
            _, at_second, is_ahead, _, live = places(lists, who, turn)

            @pl.when(is_ahead & live)
            def _():
                out[at_second] -= got[who, 2 * turn + 1]


def back_kernel(lists, got, out):
    out[...] = jnp.zeros(out.shape, F32)
    for who in range(got.shape[0]):
        for turn in range(PAIRS):
            at_first, at_second, is_ahead, differs, live = places(lists, who, turn)

            @pl.when(live)
            def _():
                out[at_first] -= got[who, 2 * turn]

            @pl.when(live & differs & jnp.logical_not(is_ahead))
            def _():
                out[at_second] -= got[who, 2 * turn + 1]


def local(orbitals, box_offsets, pair_first, pair_second, pair_count):
    members = lax.axis_size("grp")
    rows = orbitals.shape[2]
    smem = pl.BlockSpec(memory_space=pltpu.SMEM)
    vmem = pl.BlockSpec(memory_space=pltpu.VMEM)
    anywhere = pl.BlockSpec(memory_space=pl.ANY)
    limit = pltpu.CompilerParams(vmem_limit_bytes=40 * 1024 * 1024)
    hbm = pl.BlockSpec(memory_space=pltpu.HBM)
    mine = pl.pallas_call(
        entry_kernel,
        out_shape=jax.ShapeDtypeStruct((members, 1, LANES), jnp.int32),
        in_specs=[vmem] * 3,
        out_specs=vmem,
        compiler_params=limit,
        name="entry",
    )(pair_first, pair_second, pair_count)
    mine = from_behind(mine, "orb", 1)
    lists = lax.psum(mine, "grp")
    slots = 2 * PAIRS
    fields = jax.ShapeDtypeStruct((members, slots, 2, rows, CELLS), F32)
    here = pl.pallas_call(
        stage_kernel,
        out_shape=jax.ShapeDtypeStruct(orbitals.shape, F32),
        in_specs=[hbm],
        out_specs=vmem,
        compiler_params=limit,
        cost_estimate=pl.CostEstimate(flops=10**10, bytes_accessed=1 << 20, transcendentals=0),
        name="stage",
    )(pltpu.with_memory_space_constraint(orbitals, pltpu.HBM))
    behind = from_behind(here, "orb", 1)
    packed = pl.pallas_call(
        pack_kernel,
        out_shape=fields,
        in_specs=[smem, vmem, vmem],
        out_specs=vmem,
        compiler_params=limit,
        name="pack",
    )(lists, behind, here)
    got = lax.all_to_all(packed, "grp", 0, 0)
    tables = [jnp.asarray(table) for table in TABLES]
    buf = pltpu.VMEM((2, SLABS + 2 * PAD_SLABS, BOX + 2 * PAD_ROWS, LANES), F32)
    terms = pl.pallas_call(
        pair_kernel,
        out_shape=fields,
        in_specs=[smem] * 2 + [vmem] * 7,
        out_specs=vmem,
        scratch_shapes=[buf] * PAIRS,
        compiler_params=limit,
        name="pairs",
    )(box_offsets, lists, got, *tables)
    returned = lax.all_to_all(terms, "grp", 0, 0)
    shape = jax.ShapeDtypeStruct(orbitals.shape, F32)
    back_terms = pl.pallas_call(
        back_kernel,
        out_shape=shape,
        in_specs=[smem, vmem],
        out_specs=vmem,
        compiler_params=limit,
        name="back_terms",
    )(lists, returned)
    back = from_behind(back_terms, "orb", -1)
    here_terms = pl.pallas_call(
        here_kernel,
        out_shape=shape,
        in_specs=[smem, vmem],
        out_specs=vmem,
        compiler_params=limit,
        name="here_terms",
    )(lists, returned)
    return here_terms + back


def solution(mesh):
    placed = (
        P("orb", None, "grp", None),
        P(),
        P("orb", "grp", None),
        P("orb", "grp", None),
        P("orb", "grp"),
    )
    return jax.shard_map(
        local, mesh=mesh, in_specs=placed, out_specs=P("orb", None, "grp", None), check_vma=False
    )
```
